512 devices in a mesh: section: 4 (over y), dp: 16 (over z), tensor: 8 (over x, core).
Axes of the slice: x: 4, y: 4, z: 16, core: 2. Of those that a mesh axis runs over, the one named last changes fastest.
Arguments:
- hidden: bfloat16 [4, 2048, 14336], P('section', 'dp', 'tensor'), may hold values from -6 to 6
- residual_in: bfloat16 [2048, 4096], P('dp', 'tensor'), may hold values from -6 to 6
- weights: bfloat16 [4, 8, 32, 7, 128, 128], P('section', 'tensor', 'dp'), may hold values from -0.0625 to 0.0625
- kept: int32 [4, 8, 32, 7], P('section', 'tensor'), may hold values from 0 to 13, as said below
- cotangent: bfloat16 [2048, 4096], P('dp', 'tensor'), may hold values from -0.125 to 0.125
- norm_gain: float32 [4096], P('tensor'), may hold values from 0.1 to 1.9
Outputs:
- section_out: bfloat16 [4, 2048, 4096], P('section', 'dp', 'tensor')
- weight_grad: bfloat16 [4, 8, 32, 7, 128, 128], P('section', 'tensor', 'dp')
The draws below stay inside these ranges and needn't reach their ends.
Inputs may be any that keep to these rules, and one draw needn't show every extreme that they name: `kept`: for every section, tensor shard and column block, the 7 entries are distinct hidden blocks of that shard, in increasing order.
All inputs are finite; a program needn't handle non-finite values.
Results may differ from the reference program's by a relative error of at most 0.02.
Values may be sent and summed in bfloat16 or wider, within the bound.
No kernel may reach another device: no remote copies, remote signals or barrier semaphores. Data moves between devices by JAX's collectives and lax.ppermute only.
A program may use at most 64 MiB of HBM per device.

```python
import jax
import jax.numpy as jnp
from jax import lax

D = 4096
FF = 14336
BLK = 128
ROWS = 128
KEEP = 7
TOKENS = 2048
N_SECTION = 4
N_DP = 16
N_TENSOR = 8


def draw_kept(key, part):
    key = jax.random.fold_in(key, 11)
    count = N_SECTION * N_TENSOR * (D // BLK)
    keys = jax.random.split(key, count)
    orders = jax.vmap(lambda single: jax.random.permutation(single, 2 * KEEP))(keys)
    chosen = jnp.sort(orders[:, :KEEP], axis=1)
    return chosen.reshape(N_SECTION, N_TENSOR, D // BLK, KEEP).astype(jnp.int32)


def shard_levels(own_key, extent, shards, least, top_value):
    def one(axis_at, parts):
        draws = jax.random.uniform(jax.random.fold_in(jax.random.fold_in(own_key, 6), axis_at), (parts,), jnp.float32, least / len(shards), top_value / len(shards))
        return jnp.repeat(jnp.exp(draws), extent[axis_at] // parts).reshape((-1,) + (1,) * (len(extent) - axis_at - 1))

    level = one(*shards[0])
    for cut in shards[1:]:
        level = level * one(*cut)
    return level


def scatter_about(key, shape, spread, reach, cuts=(), held_as=jnp.bfloat16):
    values = spread * jax.random.normal(key, shape, jnp.float32)
    if cuts:
        values = values * shard_levels(key, shape, cuts, -0.22, 0.18)
    return jnp.clip(values, -reach, reach).astype(held_as)


def setup_inputs(seed: int = 0) -> dict:
    arg_keys = jax.random.split(jax.random.key(seed), 7)
    return {
        "hidden": scatter_about(arg_keys[0], (N_SECTION, TOKENS, FF), 1.0, 6.0, ((0, 4), (1, 16), (2, 8))),
        "residual_in": scatter_about(arg_keys[1], (TOKENS, D), 1.0, 6.0, ((0, 16), (1, 8))),
        "weights": scatter_about(arg_keys[2], (N_SECTION, N_TENSOR, D // BLK, KEEP, BLK, BLK), (FF // 2) ** -0.5, 0.0625, ((0, 4), (1, 8), (2, 16))),
        "kept": draw_kept(jax.random.fold_in(arg_keys[6], 71), 0),
        "cotangent": scatter_about(arg_keys[4], (TOKENS, D), TOKENS ** -0.5, 0.125, ((0, 16), (1, 8))),
        "norm_gain": jnp.clip(1.0 + 0.18 * jax.random.normal(arg_keys[5], (D,), jnp.float32), 0.1, 1.9),
    }


def reference(hidden, residual_in, weights, kept, cotangent, norm_gain):
    part_width = FF // N_TENSOR
    col_blocks = D // BLK
    current = residual_in
    outputs = []
    for section_num in range(N_SECTION):
        contrib = jnp.zeros((TOKENS, D), jnp.float32)
        for shard in range(N_TENSOR):
            local = hidden[section_num][:, shard * part_width:(shard + 1) * part_width]
            local = local.reshape(TOKENS, part_width // BLK, BLK)
            chosen = jnp.take(local, kept[section_num, shard], axis=1)
            partial_out = jnp.einsum('rckb,ckbd->rcd', chosen.astype(jnp.float32), weights[section_num, shard].astype(jnp.float32))
            rounded = lax.optimization_barrier(partial_out.reshape(TOKENS, D).astype(jnp.bfloat16))
            contrib = contrib + rounded.astype(jnp.float32)
        current = (current.astype(jnp.float32) + contrib).astype(jnp.bfloat16)
        outputs.append(current)
    final = current.astype(jnp.float32)
    scaled = cotangent.astype(jnp.float32) * norm_gain[None, :]
    inverse = lax.rsqrt(lax.optimization_barrier(jnp.mean(final * final, axis=1)) + 1e-05)
    mixed = lax.optimization_barrier(jnp.mean(scaled * final, axis=1))
    out_grad = (inverse[:, None] * (scaled - final * (inverse * inverse * mixed)[:, None])).astype(jnp.bfloat16)
    grad_groups = out_grad.astype(jnp.float32).reshape(N_DP, ROWS, col_blocks, BLK)
    grads = []
    for section_num in range(N_SECTION):
        shard_grads = []
        for shard in range(N_TENSOR):
            local = hidden[section_num][:, shard * part_width:(shard + 1) * part_width]
            local = local.reshape(TOKENS, part_width // BLK, BLK)
            chosen = jnp.take(local, kept[section_num, shard], axis=1).astype(jnp.float32)
            chosen = chosen.reshape(N_DP, ROWS, col_blocks, KEEP, BLK)
            per_group = jnp.einsum('prckb,prcd->pckbd', chosen, grad_groups)
            rounded = lax.optimization_barrier(per_group.astype(jnp.bfloat16))
            shard_grads.append(lax.optimization_barrier(jnp.sum(rounded.astype(jnp.float32), axis=0)).astype(jnp.bfloat16))
        grads.append(jnp.stack(shard_grads))
    return (jnp.stack(outputs), jnp.stack(grads))
```

```python
import jax
import jax.numpy as jnp
from jax import lax
from jax.sharding import PartitionSpec as P

D = 4096
PLANE = ("section", "tensor")
ALL = ("section", "dp", "tensor")


def to_columns_pairs(ns, nz, nt):
    pairs = []
    for s in range(ns):
        for p in range(nz):
            for t in range(nt):
                piece = 2 * p + s // 2
                plane = 2 * t + s % 2
                pairs.append(
                    ((s * nz + p) * nt + t, ((piece // nt) * nz + plane) * nt + piece % nt)
                )
    return pairs


def to_tokens_pairs(ns, nz, nt, turn):
    pairs = []
    for s in range(ns):
        for z in range(nz):
            for t in range(nt):
                piece = s * nt + t
                quarter = 2 * (piece % 2) + z % 2
                section = (turn + quarter) % ns
                pairs.append(
                    ((s * nz + z) * nt + t, (section * nz + piece // 2) * nt + z // 2)
                )
    return pairs


def body(hidden, residual_in, weights, kept, cotangent, norm_gain):
    ns, nz, nt = (lax.axis_size(a) for a in ALL)
    section, plane, shard = (lax.axis_index(a) for a in ALL)
    acts = hidden[0]
    blocks = weights[0, 0]
    cols, keep, blk, _ = blocks.shape
    width = cols * blk
    hidden_blocks = acts.shape[1] // blk
    every = lax.all_gather(acts, "dp", axis=0, tiled=True)
    tokens = every.shape[0]
    piece = tokens // (ns * nt)

    own_kept = lax.dynamic_slice_in_dim(kept[0, 0], plane * cols, cols, axis=0)
    hit = own_kept[None] == jnp.arange(hidden_blocks, dtype=own_kept.dtype)[:, None, None]
    dense = jnp.sum(
        jnp.where(hit[..., None, None], blocks[None].astype(jnp.float32), 0.0), axis=2
    ).astype(jnp.bfloat16)
    dense = dense.transpose(0, 2, 1, 3).reshape(hidden_blocks * blk, width)

    down, across = section // 2, section % 2
    corner = lambda a: lax.dynamic_slice(a, (down * piece, across * width), (piece, width))
    pairs = to_columns_pairs(ns, nz, nt)
    residual = lax.ppermute(corner(residual_in), ALL, pairs).astype(jnp.float32)
    scaled = corner(cotangent.astype(jnp.float32) * norm_gain[None, :])
    scaled = lax.ppermute(scaled, ALL, pairs)

    partial_out = jnp.dot(every, dense, preferred_element_type=jnp.float32).astype(jnp.bfloat16)
    received = lax.all_to_all(
        partial_out.reshape(ns * nt, piece, width), PLANE, split_axis=0, concat_axis=0, tiled=True
    )
    contrib = jnp.sum(received.reshape(ns, nt, piece, width).astype(jnp.float32), axis=1)
    outs = []
    current = residual
    for turn in range(ns):
        outs.append((current + contrib[turn]).astype(jnp.bfloat16))
        current = outs[-1].astype(jnp.float32)
    stacked = jnp.stack(outs)

    sums = jnp.concatenate([jnp.sum(current * current, axis=1), jnp.sum(scaled * current, axis=1)])
    spread = jnp.broadcast_to(sums[None, None, :], (nz, 1, 2 * piece))
    spread = lax.all_to_all(spread, "dp", split_axis=0, concat_axis=0, tiled=True)
    totals = jnp.sum(spread, axis=(0, 1)) / D
    inverse = lax.rsqrt(totals[:piece] + 1e-05)
    mixed = totals[piece:]
    out_grad = (
        inverse[:, None] * (scaled - current * (inverse * inverse * mixed)[:, None])
    ).astype(jnp.bfloat16)

    full_grad = lax.all_to_all(
        jnp.broadcast_to(out_grad[None], (ns * nt, piece, width)),
        PLANE,
        split_axis=0,
        concat_axis=0,
        tiled=True,
    ).reshape(tokens, width)

    quarter = 2 * (shard % 2) + plane % 2
    back = []
    for turn in range(ns):
        chosen = lax.dynamic_index_in_dim(stacked, (turn + quarter) % ns, 0, keepdims=False)
        back.append(lax.ppermute(chosen, ALL, to_tokens_pairs(ns, nz, nt, turn)))
    back = jnp.stack(back)
    corners = [
        lax.dynamic_index_in_dim(back, (section - q) % ns, 0, keepdims=False) for q in range(ns)
    ]
    section_out = jnp.concatenate(
        [jnp.concatenate(corners[:2], axis=1), jnp.concatenate(corners[2:], axis=1)], axis=0
    )

    grads = lax.dot_general(
        every, full_grad, (((0,), (0,)), ((), ())), preferred_element_type=jnp.float32
    ).astype(jnp.bfloat16)
    grads = grads.reshape(hidden_blocks, blk, cols, blk)
    picked = []
    for c in range(cols):
        picked.append(
            jnp.stack(
                [
                    lax.dynamic_index_in_dim(grads[:, :, c], own_kept[c, k], 0, keepdims=False)
                    for k in range(keep)
                ]
            )
        )
    return (section_out[None], jnp.stack(picked)[None, None])


def solution(mesh):
    in_specs = (
        P("section", "dp", "tensor"),
        P("dp", "tensor"),
        P("section", "tensor", "dp", None, None, None),
        P("section", "tensor", None, None),
        P("dp", "tensor"),
        P("tensor"),
    )
    out_specs = (P("section", "dp", "tensor"), P("section", "tensor", "dp", None, None, None))
    return jax.shard_map(body, mesh=mesh, in_specs=in_specs, out_specs=out_specs, check_vma=False)
```

```python
import jax
import jax.numpy as jnp
from jax import lax
from jax.experimental import pallas as pl
from jax.experimental.pallas import tpu as pltpu
from jax.sharding import PartitionSpec as P

D = 4096
PLANE = ("section", "tensor")
ALL = ("section", "dp", "tensor")


def to_columns_pairs(ns, nz, nt):
    pairs = []
    for s in range(ns):
        for p in range(nz):
            for t in range(nt):
                piece = 2 * p + s // 2
                plane = 2 * t + s % 2
                pairs.append(
                    ((s * nz + p) * nt + t, ((piece // nt) * nz + plane) * nt + piece % nt)
                )
    return pairs


def to_tokens_pairs(ns, nz, nt, turn):
    pairs = []
    for s in range(ns):
        for z in range(nz):
            for t in range(nt):
                piece = s * nt + t
                quarter = 2 * (piece % 2) + z % 2
                section = (turn + quarter) % ns
                pairs.append(
                    ((s * nz + z) * nt + t, (section * nz + piece // 2) * nt + z // 2)
                )
    return pairs


def forward_kernel(acts_ref, dense_ref, residual_ref, scaled_ref, out_ref):
    out_ref[...] = jnp.dot(
        acts_ref[...], dense_ref[...], preferred_element_type=jnp.float32
    ).astype(out_ref.dtype)


def forward(every, dense, residual, scaled):
    tokens, units = every.shape
    width = dense.shape[1]
    tile = 256
    return pl.pallas_call(
        forward_kernel,
        grid=(tokens // tile,),
        in_specs=[
            pl.BlockSpec((tile, units), lambda i: (i, 0)),
            pl.BlockSpec((units, width), lambda i: (0, 0)),
            pl.BlockSpec(memory_space=pl.ANY),
            pl.BlockSpec(memory_space=pl.ANY),
        ],
        out_specs=pl.BlockSpec((tile, width), lambda i: (i, 0)),
        out_shape=jax.ShapeDtypeStruct((tokens, width), jnp.bfloat16),
        compiler_params=pltpu.CompilerParams(vmem_limit_bytes=32 << 20),
        cost_estimate=pl.CostEstimate(
            flops=2 * tokens * units * width, bytes_accessed=2 * tokens * units, transcendentals=0
        ),
        name="forward_matmul",
    )(every, dense, residual, scaled)


def gradient_kernel(slot_ref, grad_ref, acts_ref, out_ref, turned_ref):
    step = pl.program_id(0)

    @pl.when(step == 0)
    def _():
        turned_ref[...] = grad_ref[...].T

    cols, keep, blk, _ = out_ref.shape
    per_step = acts_ref.shape[1] // blk
    found = jnp.dot(turned_ref[...], acts_ref[...], preferred_element_type=jnp.float32)
    for part in range(per_step):
        for c in range(cols):
            slot = slot_ref[c, step * per_step + part]

            @pl.when(slot >= 0)
            def _(part=part, c=c, slot=slot):
                block = found[c * blk : (c + 1) * blk, part * blk : (part + 1) * blk]
                out_ref[c, slot] = block.T.astype(out_ref.dtype)


def gradient(slots, full_grad, every, keep, blk):
    tokens, units = every.shape
    width = full_grad.shape[1]
    cols = width // blk
    per_step = 2
    return pl.pallas_call(
        gradient_kernel,
        grid_spec=pltpu.PrefetchScalarGridSpec(
            num_scalar_prefetch=1,
            grid=(units // (per_step * blk),),
            in_specs=[
                pl.BlockSpec((tokens, width), lambda i, _: (0, 0)),
                pl.BlockSpec((tokens, per_step * blk), lambda i, _: (0, i)),
            ],
            out_specs=pl.BlockSpec((cols, keep, blk, blk), lambda i, _: (0, 0, 0, 0)),
            scratch_shapes=[pltpu.VMEM((width, tokens), jnp.bfloat16)],
        ),
        out_shape=jax.ShapeDtypeStruct((cols, keep, blk, blk), jnp.bfloat16),
        compiler_params=pltpu.CompilerParams(vmem_limit_bytes=32 << 20),
        cost_estimate=pl.CostEstimate(
            flops=2 * tokens * units * width, bytes_accessed=2 * tokens * units, transcendentals=0
        ),
        name="gradient_matmul",
    )(slots, full_grad, every)


def turn_kernel(shift_ref, stacked_ref, after_ref, out_ref):
    ns = stacked_ref.shape[0]
    for turn in range(ns):
        out_ref[turn] = stacked_ref[lax.rem(turn + shift_ref[0], ns)]


def turned(shift, stacked, after):
    return pl.pallas_call(
        turn_kernel,
        grid_spec=pltpu.PrefetchScalarGridSpec(
            num_scalar_prefetch=1,
            grid=(1,),
            in_specs=[
                pl.BlockSpec(stacked.shape, lambda i, _: (0, 0, 0)),
                pl.BlockSpec(memory_space=pl.ANY),
            ],
            out_specs=pl.BlockSpec(stacked.shape, lambda i, _: (0, 0, 0)),
        ),
        out_shape=jax.ShapeDtypeStruct(stacked.shape, stacked.dtype),
        name="turn_sections",
    )(shift, stacked, after)


def body(hidden, residual_in, weights, kept, cotangent, norm_gain):
    ns, nz, nt = (lax.axis_size(a) for a in ALL)
    section, plane, shard = (lax.axis_index(a) for a in ALL)
    acts = hidden[0]
    blocks = weights[0, 0]
    cols, keep, blk, _ = blocks.shape
    width = cols * blk
    hidden_blocks = acts.shape[1] // blk
    every = lax.all_gather(acts, "dp", axis=0, tiled=True)
    tokens = every.shape[0]
    piece = tokens // (ns * nt)

    own_kept = lax.dynamic_slice_in_dim(kept[0, 0], plane * cols, cols, axis=0)
    hit = own_kept[None] == jnp.arange(hidden_blocks, dtype=own_kept.dtype)[:, None, None]
    dense = jnp.sum(
        jnp.where(hit[..., None, None], blocks[None].astype(jnp.float32), 0.0), axis=2
    ).astype(jnp.bfloat16)
    dense = dense.transpose(0, 2, 1, 3).reshape(hidden_blocks * blk, width)

    down, across = section // 2, section % 2
    corner = lambda a: lax.dynamic_slice(a, (down * piece, across * width), (piece, width))
    pairs = to_columns_pairs(ns, nz, nt)
    residual = lax.ppermute(corner(residual_in), ALL, pairs)
    scaled = corner(cotangent.astype(jnp.float32) * norm_gain[None, :])
    scaled = lax.ppermute(scaled, ALL, pairs)

    partial_out = forward(every, dense, residual, scaled)
    received = lax.all_to_all(
        partial_out.reshape(ns * nt, piece, width), PLANE, split_axis=0, concat_axis=0, tiled=True
    )
    contrib = jnp.sum(received.reshape(ns, nt, piece, width).astype(jnp.float32), axis=1)
    outs = []
    current = residual.astype(jnp.float32)
    for turn in range(ns):
        outs.append((current + contrib[turn]).astype(jnp.bfloat16))
        current = outs[-1].astype(jnp.float32)
    stacked = jnp.stack(outs)

    sums = jnp.concatenate([jnp.sum(current * current, axis=1), jnp.sum(scaled * current, axis=1)])
    spread = jnp.broadcast_to(sums[None, None, :], (nz, 1, 2 * piece))
    spread = lax.all_to_all(spread, "dp", split_axis=0, concat_axis=0, tiled=True)
    totals = jnp.sum(spread, axis=(0, 1)) / D
    inverse = lax.rsqrt(totals[:piece] + 1e-05)
    mixed = totals[piece:]
    out_grad = (
        inverse[:, None] * (scaled - current * (inverse * inverse * mixed)[:, None])
    ).astype(jnp.bfloat16)

    full_grad = lax.all_to_all(
        jnp.broadcast_to(out_grad[None], (ns * nt, piece, width)),
        PLANE,
        split_axis=0,
        concat_axis=0,
        tiled=True,
    ).reshape(tokens, width)

    quarter = 2 * (shard % 2) + plane % 2
    sent = turned(quarter.astype(jnp.int32).reshape(1), stacked, full_grad)
    back = [lax.ppermute(sent[turn], ALL, to_tokens_pairs(ns, nz, nt, turn)) for turn in range(ns)]
    back = jnp.stack(back)
    corners = [
        lax.dynamic_index_in_dim(back, (section - q) % ns, 0, keepdims=False) for q in range(ns)
    ]
    section_out = jnp.concatenate(
        [jnp.concatenate(corners[:2], axis=1), jnp.concatenate(corners[2:], axis=1)], axis=0
    )

    found = jnp.any(hit, axis=2)
    slots = jnp.where(found, jnp.argmax(hit, axis=2), -1).T.astype(jnp.int32)
    grads = gradient(slots, full_grad, every, keep, blk)
    return (section_out[None], grads[None, None])


def solution(mesh):
    in_specs = (
        P("section", "dp", "tensor"),
        P("dp", "tensor"),
        P("section", "tensor", "dp", None, None, None),
        P("section", "tensor", None, None),
        P("dp", "tensor"),
        P("tensor"),
    )
    out_specs = (P("section", "dp", "tensor"), P("section", "tensor", "dp", None, None, None))
    return jax.shard_map(body, mesh=mesh, in_specs=in_specs, out_specs=out_specs, check_vma=False)
```

```python
import jax
import jax.numpy as jnp
from jax import lax
from jax.experimental import pallas as pl
from jax.experimental.pallas import tpu as pltpu
from jax.sharding import PartitionSpec as P

D = 4096
PLANE = ("section", "tensor")
ALL = ("section", "dp", "tensor")
VMEM = 56 << 20
HALF = 4


def regroup(even, odd):
    upper = lax.broadcasted_iota(jnp.int32, even.shape, even.ndim - 2) < HALF
    axis = even.ndim - 2
    first = jnp.where(upper, even, pltpu.roll(odd, HALF, axis))
    second = jnp.where(upper, pltpu.roll(even, HALF, axis), odd)
    return first, second


def call(kernel, name, flops, moved, **kwargs):
    return pl.pallas_call(
        kernel,
        compiler_params=pltpu.CompilerParams(vmem_limit_bytes=VMEM),
        cost_estimate=pl.CostEstimate(flops=flops, bytes_accessed=moved, transcendentals=0),
        name=name,
        **kwargs,
    )


def forward_kernel(acts_ref, dense_ref, residual_ref, cot_ref, gain_ref, out_ref):
    found = jnp.dot(acts_ref[...], dense_ref[...], preferred_element_type=jnp.float32)
    rows = found.shape[0] // 4
    groups = [
        found[q * rows : (q + 1) * rows].reshape(rows // 8, 8, found.shape[1]) for q in range(4)
    ]
    left, right = regroup(*groups[:2]), regroup(*groups[2:])
    for parity in range(2):
        joined = jnp.concatenate([left[parity], right[parity]], axis=1)
        out_ref[:, parity] = joined.astype(out_ref.dtype)


def forward(every, dense, rows, after):
    tokens, units = every.shape
    width = dense.shape[1]
    groups = tokens // rows
    pairs = rows // 8
    out = call(
        forward_kernel,
        "forward_matmul",
        2 * tokens * units * width,
        2 * tokens * units,
        grid=(groups // 4,),
        in_specs=[
            pl.BlockSpec((4 * rows, units), lambda i: (i, 0)),
            pl.BlockSpec((units, width), lambda i: (0, 0)),
        ]
        + [pl.BlockSpec(memory_space=pl.ANY)] * 3,
        out_specs=pl.BlockSpec((pairs, 2, 16, width), lambda i: (0, 0, i, 0)),
        out_shape=jax.ShapeDtypeStruct((pairs, 2, HALF * groups, width), jnp.bfloat16),
    )(every, dense, *after)
    return out.reshape(2 * pairs, HALF * groups, width)


def cascade_kernel(parts_ref, residual_ref, cot_ref, gain_ref, out_ref, final_ref, scaled_ref):
    shards = parts_ref.shape[0] // 4
    rows, width = residual_ref.shape
    current = residual_ref[...].astype(jnp.float32)
    tiles = []
    for section in range(4):
        contrib = parts_ref[section * shards].astype(jnp.float32)
        for shard in range(1, shards):
            contrib += parts_ref[section * shards + shard].astype(jnp.float32)
        current = (current + contrib).astype(jnp.bfloat16).astype(jnp.float32)
        tiles.append(current.reshape(rows // 8, 8, width))
    scaled = cot_ref[...].astype(jnp.float32) * gain_ref[...]
    final_ref[...] = current
    scaled_ref[...] = scaled

    lane = lax.broadcasted_iota(jnp.int32, (rows, 128), 1)
    table = jnp.zeros((rows, 128), jnp.float32)
    for at, factor in enumerate((current, scaled)):
        left = jnp.sum(factor * current, axis=1, keepdims=True)
        for term in range(3):
            head = left.astype(jnp.bfloat16).astype(jnp.float32)
            table = jnp.where(lane == 3 * at + term, head, table)
            left = left - head
    table = jnp.concatenate([table, jnp.zeros((width - rows, 128), jnp.float32)], axis=0)
    sums = jnp.broadcast_to(table.T[None, :8], (rows // 8, 8, width))

    low, high = regroup(*tiles[:2]), regroup(*tiles[2:])
    for parity in range(2):
        joined = jnp.concatenate([low[parity], high[parity], sums], axis=1)
        out_ref[:, parity] = joined.astype(out_ref.dtype)


def cascade(parts, residual, cotangent, gain):
    rows, width = residual.shape
    half = jax.ShapeDtypeStruct((rows, width), jnp.float32)
    out, final, scaled = call(
        cascade_kernel,
        "cascade",
        parts.size,
        2 * parts.size,
        out_shape=(
            jax.ShapeDtypeStruct((rows // 8, 2, 24, width), jnp.bfloat16),
            half,
            half,
        ),
    )(parts, residual, cotangent, gain)
    return out.reshape(rows // 4, 24, width), final, scaled


def norm_kernel(got_ref, final_ref, scaled_ref, out_ref):
    planes = got_ref.shape[0]
    rows, width = final_ref.shape
    sums = got_ref[0, 16:24].astype(jnp.float32)
    for plane in range(1, planes):
        sums += got_ref[plane, 16:24].astype(jnp.float32)
    table = jnp.concatenate([sums, jnp.zeros((120, width), jnp.float32)], axis=0).T[:rows]
    lane = lax.broadcasted_iota(jnp.int32, table.shape, 1)
    square = jnp.sum(jnp.where(lane < 3, table, 0.0), axis=1, keepdims=True) / D
    mixed = jnp.sum(jnp.where(lane < 3, 0.0, table), axis=1, keepdims=True) / D
    inverse = lax.rsqrt(square + 1e-05)
    grad = inverse * (scaled_ref[...] - final_ref[...] * (inverse * inverse * mixed))

    shards = planes // 2
    spread = jnp.broadcast_to(grad[None], (shards, rows, width))
    pairs = got_ref[...].astype(jnp.float32).reshape(shards, 2, 24, width)
    for at in range(2):
        part = slice(8 * at, 8 * at + 8)
        for parity, tile in enumerate(regroup(pairs[:, 0, part], pairs[:, 1, part])):
            joined = jnp.concatenate([spread, tile], axis=1)
            out_ref[2 * at + parity] = joined.astype(out_ref.dtype)


def norm(got, final, scaled):
    rows, width = final.shape
    shards = got.shape[0] // 2
    out = call(
        norm_kernel,
        "norm_gradient",
        got.size,
        4 * got.size,
        out_shape=jax.ShapeDtypeStruct((4, shards, rows + 8, width), jnp.bfloat16),
    )(got, final, scaled)
    return out.reshape(4 * shards, rows + 8, width)


def gradient_kernel(slot_ref, full_ref, acts_ref, out_ref, section_ref, turned_ref):
    step = pl.program_id(0)
    cols, keep, blk, _ = out_ref.shape
    pairs, _, rows, width = full_ref.shape

    @pl.when(step == 0)
    def _():
        def tiles(at):
            even = full_ref[:, 0, at : at + 8].astype(jnp.float32)
            odd = full_ref[:, 1, at : at + 8].astype(jnp.float32)
            return [t.reshape(pairs * 8, width) for t in regroup(even, odd)]

        for two in range((rows - 8) // 8):
            for parity, tile in enumerate(tiles(8 * two)):
                at = (2 * two + parity) * pairs * 8
                turned_ref[:, at : at + pairs * 8] = tile.T.astype(turned_ref.dtype)
        for parity, tile in enumerate(tiles(rows - 8)):
            section_ref[:, parity * width : (parity + 1) * width] = tile.astype(section_ref.dtype)

    per_step = acts_ref.shape[1] // blk
    found = jnp.dot(turned_ref[...], acts_ref[...], preferred_element_type=jnp.float32)
    for part in range(per_step):
        for c in range(cols):
            slot = slot_ref[c, step * per_step + part]

            @pl.when(slot >= 0)
            def _(part=part, c=c, slot=slot):
                block = found[c * blk : (c + 1) * blk, part * blk : (part + 1) * blk]
                out_ref[c, slot] = block.T.astype(out_ref.dtype)


def gradient(slots, full, every, keep, blk):
    tokens, units = every.shape
    devices, rows, width = full.shape
    cols = width // blk
    per_step = 2
    return call(
        gradient_kernel,
        "gradient_matmul",
        2 * tokens * units * width,
        2 * tokens * units,
        grid_spec=pltpu.PrefetchScalarGridSpec(
            num_scalar_prefetch=1,
            grid=(units // (per_step * blk),),
            in_specs=[
                pl.BlockSpec((devices // 2, 2, rows, width), lambda i, _: (0, 0, 0, 0)),
                pl.BlockSpec((tokens, per_step * blk), lambda i, _: (0, i)),
            ],
            out_specs=[
                pl.BlockSpec((cols, keep, blk, blk), lambda i, _: (0, 0, 0, 0)),
                pl.BlockSpec((devices * HALF, 2 * width), lambda i, _: (0, 0)),
            ],
            scratch_shapes=[pltpu.VMEM((width, tokens), jnp.bfloat16)],
        ),
        out_shape=(
            jax.ShapeDtypeStruct((cols, keep, blk, blk), jnp.bfloat16),
            jax.ShapeDtypeStruct((devices * HALF, 2 * width), jnp.bfloat16),
        ),
    )(slots, full.reshape(devices // 2, 2, rows, width), every)


def exchange(value, axes):
    return lax.all_to_all(value, axes, split_axis=0, concat_axis=0, tiled=True)


def body(hidden, residual_in, weights, kept, cotangent, norm_gain):
    ns, nz, nt = (lax.axis_size(a) for a in ALL)
    section, plane = lax.axis_index("section"), lax.axis_index("dp")
    acts = hidden[0]
    rows = acts.shape[0]
    blocks = weights[0, 0]
    cols, keep, blk, _ = blocks.shape
    width = cols * blk
    hidden_blocks = acts.shape[1] // blk
    every = lax.all_gather(acts, "dp", axis=0, tiled=True)

    own_kept = lax.dynamic_slice_in_dim(kept[0, 0], plane * cols, cols, axis=0)
    hit = own_kept[None] == jnp.arange(hidden_blocks, dtype=own_kept.dtype)[:, None, None]
    dense = jnp.sum(
        jnp.where(hit[..., None, None], blocks[None].astype(jnp.float32), 0.0), axis=2
    ).astype(jnp.bfloat16)
    dense = dense.transpose(0, 2, 1, 3).reshape(hidden_blocks * blk, width)
    slots = jnp.where(jnp.any(hit, axis=2), jnp.argmax(hit, axis=2), -1).T.astype(jnp.int32)

    both = jnp.stack([residual_in, cotangent])
    piece = both.shape[2] // ns
    both = lax.dynamic_slice_in_dim(both, section * piece, piece, axis=2)
    both = both.reshape(2, ns * nt, HALF, piece).transpose(1, 0, 2, 3)
    both = exchange(both.reshape(ns * nt, 2 * HALF, piece), PLANE)
    both = both.reshape(2, 2, nt, 2 * HALF, piece).transpose(2, 0, 3, 1, 4)
    both = exchange(both.reshape(nz, 2 * HALF, width), "dp")
    both = both.reshape(nz, 2, HALF, width).transpose(1, 0, 2, 3).reshape(2, nz * HALF, width)
    residual, cot = both[0], both[1]
    gain = lax.all_gather(norm_gain, "tensor", axis=0, tiled=True)
    gain = lax.dynamic_slice_in_dim(gain, plane * width, width).reshape(1, width)

    partial_out = forward(every, dense, rows, (residual, cot, gain))
    parts = exchange(partial_out, PLANE)
    sent, final, scaled = cascade(parts, residual, cot, gain)
    spread = norm(exchange(sent, "dp"), final, scaled)
    grads, section_out = gradient(slots, exchange(spread, PLANE), every, keep, blk)
    return (section_out[None], grads[None, None])


def solution(mesh):
    in_specs = (
        P("section", "dp", "tensor"),
        P("dp", "tensor"),
        P("section", "tensor", "dp", None, None, None),
        P("section", "tensor", None, None),
        P("dp", "tensor"),
        P("tensor"),
    )
    out_specs = (P("section", "dp", "tensor"), P("section", "tensor", "dp", None, None, None))
    return jax.shard_map(body, mesh=mesh, in_specs=in_specs, out_specs=out_specs, check_vma=False)
```

```python
import jax
import jax.numpy as jnp
from jax import lax
from jax.experimental import pallas as pl
from jax.experimental.pallas import tpu as pltpu
from jax.sharding import PartitionSpec as P

D = 4096
PLANE = ("section", "tensor")
ALL = ("section", "dp", "tensor")
MOST_VMEM = 56 << 20
HALF = 4


def regroup(even, odd):
    upper = lax.broadcasted_iota(jnp.int32, even.shape, even.ndim - 2) < HALF
    axis = even.ndim - 2
    first = jnp.where(upper, even, pltpu.roll(odd, HALF, axis))
    second = jnp.where(upper, pltpu.roll(even, HALF, axis), odd)
    return first, second


def call(kernel, name, flops, moved, vmem=16 << 20, **kwargs):
    return pl.pallas_call(
        kernel,
        compiler_params=pltpu.CompilerParams(vmem_limit_bytes=vmem),
        cost_estimate=pl.CostEstimate(flops=flops, bytes_accessed=moved, transcendentals=0),
        name=name,
        **kwargs,
    )


def split_kernel(section_ref, residual_ref, cot_ref, gain_ref, out_ref):
    rows, width = residual_ref.shape
    shape = (rows // 8, 8, width)
    scaled = cot_ref[...].astype(jnp.float32) * gain_ref[...]
    tiles = regroup(residual_ref[...].astype(jnp.float32).reshape(shape), scaled.reshape(shape))
    for parity in range(2):
        out_ref[:, parity] = tiles[parity].astype(out_ref.dtype)


def split(section, residual, cotangent, gain):
    rows, width = residual.shape
    part = width // lax.axis_size("section")
    block = pl.BlockSpec((rows, part), lambda i, section: (0, section[0]))
    out = call(
        split_kernel,
        "split_rows",
        rows * part,
        6 * rows * part,
        grid_spec=pltpu.PrefetchScalarGridSpec(
            num_scalar_prefetch=1,
            grid=(1,),
            in_specs=[
                block,
                block,
                pl.BlockSpec((1, part), lambda i, section: (0, section[0])),
            ],
            out_specs=pl.BlockSpec((rows // 8, 2, 8, part), lambda i, section: (0, 0, 0, 0)),
        ),
        out_shape=jax.ShapeDtypeStruct((rows // 8, 2, 8, part), jnp.bfloat16),
    )(section.astype(jnp.int32).reshape(1), residual, cotangent, gain.reshape(1, width))
    return out.reshape(rows // 4, 8, part)


def join_kernel(got_ref, out_ref):
    part = got_ref.shape[2]
    shards = out_ref.shape[0] // 2
    for half in range(2):
        for shard in range(shards):
            for side in range(2):
                tile = got_ref[(2 * half + side) * shards + shard]
                out_ref[2 * shard + half, :, side * part : (side + 1) * part] = tile


def join(got, planes):
    _, rows, part = got.shape
    shape = (planes, rows, 2 * part)
    return call(
        join_kernel,
        "join_columns",
        got.size,
        4 * got.size,
        grid=(1,),
        in_specs=[pl.BlockSpec(got.shape, lambda i: (0, 0, 0))],
        out_specs=pl.BlockSpec(shape, lambda i: (0, 0, 0)),
        out_shape=jax.ShapeDtypeStruct(shape, got.dtype),
    )(got)


def forward_kernel(acts_ref, dense_ref, after_ref, out_ref):
    found = jnp.dot(acts_ref[...], dense_ref[...], preferred_element_type=jnp.float32)
    rows = found.shape[0] // 4
    groups = [
        found[q * rows : (q + 1) * rows].reshape(rows // 8, 8, found.shape[1]) for q in range(4)
    ]
    left, right = regroup(*groups[:2]), regroup(*groups[2:])
    for parity in range(2):
        joined = jnp.concatenate([left[parity], right[parity]], axis=1)
        out_ref[:, parity] = joined.astype(out_ref.dtype)


def forward(every, dense, rows, after):
    tokens, units = every.shape
    width = dense.shape[1]
    groups = tokens // rows
    pairs = rows // 8
    out = call(
        forward_kernel,
        "forward_matmul",
        2 * tokens * units * width,
        2 * tokens * units,
        MOST_VMEM,
        grid=(groups // 4,),
        in_specs=[
            pl.BlockSpec((4 * rows, units), lambda i: (i, 0)),
            pl.BlockSpec((units, width), lambda i: (0, 0)),
        ]
        + [pl.BlockSpec(memory_space=pl.ANY)],
        out_specs=pl.BlockSpec((pairs, 2, 16, width), lambda i: (0, 0, i, 0)),
        out_shape=jax.ShapeDtypeStruct((pairs, 2, HALF * groups, width), jnp.bfloat16),
    )(every, dense, after)
    return out.reshape(2 * pairs, HALF * groups, width)


def cascade_kernel(parts_ref, start_ref, out_ref, final_ref, scaled_ref):
    rows, width = final_ref.shape
    shards = parts_ref.shape[0] // 4
    start = start_ref[...].astype(jnp.float32).reshape(rows // 8, 2, 8, width)
    current, scaled = (t.reshape(rows, width) for t in regroup(start[:, 0], start[:, 1]))
    tiles = []
    for section in range(4):
        contrib = parts_ref[section * shards].astype(jnp.float32)
        for shard in range(1, shards):
            contrib += parts_ref[section * shards + shard].astype(jnp.float32)
        current = (current + contrib).astype(jnp.bfloat16).astype(jnp.float32)
        tiles.append(current.reshape(rows // 8, 8, width))
    final_ref[...] = current
    scaled_ref[...] = scaled

    lane = lax.broadcasted_iota(jnp.int32, (rows, 128), 1)
    table = jnp.zeros((rows, 128), jnp.float32)
    for at, factor in enumerate((current, scaled)):
        left = jnp.sum(factor * current, axis=1, keepdims=True)
        for term in range(3):
            head = left.astype(jnp.bfloat16).astype(jnp.float32)
            table = jnp.where(lane == 3 * at + term, head, table)
            left = left - head
    table = jnp.concatenate([table, jnp.zeros((width - rows, 128), jnp.float32)], axis=0)
    sums = jnp.broadcast_to(table.T[None, :8], (rows // 8, 8, width))

    low, high = regroup(*tiles[:2]), regroup(*tiles[2:])
    for parity in range(2):
        joined = jnp.concatenate([low[parity], high[parity], sums], axis=1)
        out_ref[:, parity] = joined.astype(out_ref.dtype)


def cascade(parts, start):
    _, rows, width = parts.shape
    half = jax.ShapeDtypeStruct((rows, width), jnp.float32)
    out, final, scaled = call(
        cascade_kernel,
        "cascade",
        parts.size,
        2 * parts.size,
        out_shape=(jax.ShapeDtypeStruct((rows // 8, 2, 24, width), jnp.bfloat16), half, half),
    )(parts, start)
    return out.reshape(rows // 4, 24, width), final, scaled


def norm_kernel(got_ref, final_ref, scaled_ref, out_ref):
    planes = got_ref.shape[0]
    rows, width = final_ref.shape
    sums = got_ref[0, 16:24].astype(jnp.float32)
    for plane in range(1, planes):
        sums += got_ref[plane, 16:24].astype(jnp.float32)
    table = jnp.concatenate([sums, jnp.zeros((120, width), jnp.float32)], axis=0).T[:rows]
    lane = lax.broadcasted_iota(jnp.int32, table.shape, 1)
    square = jnp.sum(jnp.where(lane < 3, table, 0.0), axis=1, keepdims=True) / D
    mixed = jnp.sum(jnp.where(lane < 3, 0.0, table), axis=1, keepdims=True) / D
    inverse = lax.rsqrt(square + 1e-05)
    grad = inverse * (scaled_ref[...] - final_ref[...] * (inverse * inverse * mixed))

    shards = planes // 2
    spread = jnp.broadcast_to(grad[None], (shards, rows, width))
    pairs = got_ref[...].astype(jnp.float32).reshape(shards, 2, 24, width)
    for at in range(2):
        part = slice(8 * at, 8 * at + 8)
        for parity, tile in enumerate(regroup(pairs[:, 0, part], pairs[:, 1, part])):
            joined = jnp.concatenate([spread, tile], axis=1)
            out_ref[2 * at + parity] = joined.astype(out_ref.dtype)


def norm(got, final, scaled):
    rows, width = final.shape
    shards = got.shape[0] // 2
    out = call(
        norm_kernel,
        "norm_gradient",
        got.size,
        4 * got.size,
        out_shape=jax.ShapeDtypeStruct((4, shards, rows + 8, width), jnp.bfloat16),
    )(got, final, scaled)
    return out.reshape(4 * shards, rows + 8, width)


def gradient_kernel(
    slot_ref, full_ref, acts_ref, out_ref, section_ref, turned_ref, held_ref, sems
):
    step = pl.program_id(0)
    cols, keep, blk, _ = out_ref.shape
    pairs, _, rows, width = full_ref.shape
    chunks, _, piece = held_ref.shape

    def fetch(chunk):
        start = pl.multiple_of(chunk * piece, piece)
        return pltpu.make_async_copy(
            acts_ref.at[:, pl.ds(start, piece)], held_ref.at[chunk], sems.at[chunk]
        )

    @pl.when(step == 0)
    def _():
        for chunk in range(chunks):
            fetch(chunk).start()

        def tiles(at):
            even = full_ref[:, 0, at : at + 8].astype(jnp.float32)
            odd = full_ref[:, 1, at : at + 8].astype(jnp.float32)
            return [t.reshape(pairs * 8, width) for t in regroup(even, odd)]

        for two in range((rows - 8) // 8):
            for parity, tile in enumerate(tiles(8 * two)):
                at = (2 * two + parity) * pairs * 8
                turned_ref[:, at : at + pairs * 8] = tile.T.astype(turned_ref.dtype)
        for parity, tile in enumerate(tiles(rows - 8)):
            section_ref[:, parity * width : (parity + 1) * width] = tile.astype(section_ref.dtype)

    per_step = piece // blk
    fetch(step).wait()
    found = jnp.dot(turned_ref[...], held_ref[step], preferred_element_type=jnp.float32)
    for part in range(per_step):
        for c in range(cols):
            slot = slot_ref[c, step * per_step + part]

            @pl.when(slot >= 0)
            def _(part=part, c=c, slot=slot):
                block = found[c * blk : (c + 1) * blk, part * blk : (part + 1) * blk]
                out_ref[c, slot] = block.T.astype(out_ref.dtype)


def gradient(slots, full, every, keep, blk):
    tokens, units = every.shape
    devices, rows, width = full.shape
    cols = width // blk
    per_step = 2
    return call(
        gradient_kernel,
        "gradient_matmul",
        2 * tokens * units * width,
        2 * tokens * units,
        MOST_VMEM,
        grid_spec=pltpu.PrefetchScalarGridSpec(
            num_scalar_prefetch=1,
            grid=(units // (per_step * blk),),
            in_specs=[
                pl.BlockSpec((devices // 2, 2, rows, width), lambda i, _: (0, 0, 0, 0)),
                pl.BlockSpec(memory_space=pl.ANY),
            ],
            out_specs=[
                pl.BlockSpec((cols, keep, blk, blk), lambda i, _: (0, 0, 0, 0)),
                pl.BlockSpec((devices * HALF, 2 * width), lambda i, _: (0, 0)),
            ],
            scratch_shapes=[
                pltpu.VMEM((width, tokens), jnp.bfloat16),
                pltpu.VMEM((units // (per_step * blk), tokens, per_step * blk), every.dtype),
                pltpu.SemaphoreType.DMA((units // (per_step * blk),)),
            ],
        ),
        out_shape=(
            jax.ShapeDtypeStruct((cols, keep, blk, blk), jnp.bfloat16),
            jax.ShapeDtypeStruct((devices * HALF, 2 * width), jnp.bfloat16),
        ),
    )(slots, full.reshape(devices // 2, 2, rows, width), every)


def exchange(value, axes):
    return lax.all_to_all(value, axes, split_axis=0, concat_axis=0, tiled=True)


def body(hidden, residual_in, weights, kept, cotangent, norm_gain):
    ns, nz, nt = (lax.axis_size(a) for a in ALL)
    section, plane = lax.axis_index("section"), lax.axis_index("dp")
    acts = hidden[0]
    rows = acts.shape[0]
    blocks = weights[0, 0]
    cols, keep, blk, _ = blocks.shape
    width = cols * blk
    hidden_blocks = acts.shape[1] // blk
    every = lax.all_gather(acts, "dp", axis=0, tiled=True)
    own_kept = lax.dynamic_slice_in_dim(kept[0, 0], plane * cols, cols, axis=0)
    hit = own_kept[None] == jnp.arange(hidden_blocks, dtype=own_kept.dtype)[:, None, None]
    dense = jnp.sum(
        jnp.where(hit[..., None, None], blocks[None].astype(jnp.float32), 0.0), axis=2
    ).astype(jnp.bfloat16)
    dense = dense.transpose(0, 2, 1, 3).reshape(hidden_blocks * blk, width)
    slots = jnp.where(jnp.any(hit, axis=2), jnp.argmax(hit, axis=2), -1).T.astype(jnp.int32)

    start = exchange(split(section, residual_in, cotangent, norm_gain), PLANE)
    start = exchange(join(start, nz), "dp")
    parts = exchange(forward(every, dense, rows, start), PLANE)
    sent, final, scaled = cascade(parts, start)
    spread = norm(exchange(sent, "dp"), final, scaled)
    grads, section_out = gradient(slots, exchange(spread, PLANE), every, keep, blk)
    return (section_out[None], grads[None, None])


def solution(mesh):
    in_specs = (
        P("section", "dp", "tensor"),
        P("dp", "tensor"),
        P("section", "tensor", "dp", None, None, None),
        P("section", "tensor", None, None),
        P("dp", "tensor"),
        P("tensor"),
    )
    out_specs = (P("section", "dp", "tensor"), P("section", "tensor", "dp", None, None, None))
    return jax.shard_map(body, mesh=mesh, in_specs=in_specs, out_specs=out_specs, check_vma=False)
```

```python
import jax
import jax.numpy as jnp
from jax import lax
from jax.experimental import pallas as pl
from jax.experimental.pallas import tpu as pltpu
from jax.sharding import PartitionSpec as P

D = 4096
PLANE = ("section", "tensor")
ALL = ("section", "dp", "tensor")
HALF = 4


def regroup(even, odd):
    upper = lax.broadcasted_iota(jnp.int32, even.shape, even.ndim - 2) < HALF
    axis = even.ndim - 2
    first = jnp.where(upper, even, pltpu.roll(odd, HALF, axis))
    second = jnp.where(upper, pltpu.roll(even, HALF, axis), odd)
    return first, second


def call(kernel, name, flops, moved, vmem=16 << 20, **kwargs):
    return pl.pallas_call(
        kernel,
        compiler_params=pltpu.CompilerParams(vmem_limit_bytes=vmem),
        cost_estimate=pl.CostEstimate(flops=flops, bytes_accessed=moved, transcendentals=0),
        name=name,
        **kwargs,
    )


def split_kernel(section_ref, residual_ref, cot_ref, gain_ref, out_ref):
    rows, width = residual_ref.shape
    shape = (rows // 8, 8, width)
    scaled = cot_ref[...].astype(jnp.float32) * gain_ref[...]
    tiles = regroup(residual_ref[...].astype(jnp.float32).reshape(shape), scaled.reshape(shape))
    for parity in range(2):
        out_ref[:, parity] = tiles[parity].astype(out_ref.dtype)


def split(section, residual, cotangent, gain):
    rows, width = residual.shape
    part = width // lax.axis_size("section")
    block = pl.BlockSpec((rows, part), lambda i, section: (0, section[0]))
    out = call(
        split_kernel,
        "split_rows",
        rows * part,
        6 * rows * part,
        grid_spec=pltpu.PrefetchScalarGridSpec(
            num_scalar_prefetch=1,
            grid=(1,),
            in_specs=[
                block,
                block,
                pl.BlockSpec((1, part), lambda i, section: (0, section[0])),
            ],
            out_specs=pl.BlockSpec((rows // 8, 2, 8, part), lambda i, section: (0, 0, 0, 0)),
        ),
        out_shape=jax.ShapeDtypeStruct((rows // 8, 2, 8, part), jnp.bfloat16),
    )(section.astype(jnp.int32).reshape(1), residual, cotangent, gain.reshape(1, width))
    return out.reshape(rows // 4, 8, part)


def join_kernel(got_ref, out_ref):
    part = got_ref.shape[2]
    shards = out_ref.shape[0] // 2
    for half in range(2):
        for shard in range(shards):
            for side in range(2):
                tile = got_ref[(2 * half + side) * shards + shard]
                out_ref[2 * shard + half, :, side * part : (side + 1) * part] = tile


def join(got, planes):
    _, rows, part = got.shape
    shape = (planes, rows, 2 * part)
    return call(
        join_kernel,
        "join_columns",
        got.size,
        4 * got.size,
        grid=(1,),
        in_specs=[pl.BlockSpec(got.shape, lambda i: (0, 0, 0))],
        out_specs=pl.BlockSpec(shape, lambda i: (0, 0, 0)),
        out_shape=jax.ShapeDtypeStruct(shape, got.dtype),
    )(got)


def forward_kernel(acts_ref, dense_ref, after_ref, out_ref, held_ref):
    pairs, _, _, width = out_ref.shape
    rows = 8 * pairs
    for step in range(acts_ref.shape[0] // (4 * rows)):
        acts = acts_ref[4 * step * rows : 4 * (step + 1) * rows]
        held_ref[4 * step * rows : 4 * (step + 1) * rows] = acts
        found = jnp.dot(acts, dense_ref[...], preferred_element_type=jnp.float32)
        groups = [found[q * rows : (q + 1) * rows].reshape(pairs, 8, width) for q in range(4)]
        left, right = regroup(*groups[:2]), regroup(*groups[2:])
        for parity in range(2):
            joined = jnp.concatenate([left[parity], right[parity]], axis=1)
            out_ref[:, parity, 16 * step : 16 * (step + 1)] = joined.astype(out_ref.dtype)


def forward(every, dense, rows, after):
    tokens, units = every.shape
    width = dense.shape[1]
    groups = tokens // rows
    pairs = rows // 8
    whole = pl.BlockSpec(memory_space=pltpu.VMEM)
    out, held = call(
        forward_kernel,
        "forward_matmul",
        2 * tokens * units * width,
        2 * tokens * units,
        in_specs=[whole, whole, pl.BlockSpec(memory_space=pl.ANY)],
        out_specs=[whole, whole],
        out_shape=(
            jax.ShapeDtypeStruct((pairs, 2, HALF * groups, width), jnp.bfloat16),
            pltpu.VMEM(every.shape, every.dtype),
        ),
    )(every, dense, after)
    return out.reshape(2 * pairs, HALF * groups, width), held


def cascade_kernel(parts_ref, start_ref, out_ref, final_ref, scaled_ref):
    rows, width = final_ref.shape
    shards = parts_ref.shape[0] // 4
    start = start_ref[...].astype(jnp.float32).reshape(rows // 8, 2, 8, width)
    current, scaled = (t.reshape(rows, width) for t in regroup(start[:, 0], start[:, 1]))
    tiles = []
    for section in range(4):
        contrib = parts_ref[section * shards].astype(jnp.float32)
        for shard in range(1, shards):
            contrib += parts_ref[section * shards + shard].astype(jnp.float32)
        current = (current + contrib).astype(jnp.bfloat16).astype(jnp.float32)
        tiles.append(current.reshape(rows // 8, 8, width))
    final_ref[...] = current
    scaled_ref[...] = scaled

    lane = lax.broadcasted_iota(jnp.int32, (rows, 128), 1)
    table = jnp.zeros((rows, 128), jnp.float32)
    for at, factor in enumerate((current, scaled)):
        left = jnp.sum(factor * current, axis=1, keepdims=True)
        for term in range(3):
            head = left.astype(jnp.bfloat16).astype(jnp.float32)
            table = jnp.where(lane == 3 * at + term, head, table)
            left = left - head
    table = jnp.concatenate([table, jnp.zeros((width - rows, 128), jnp.float32)], axis=0)
    sums = jnp.broadcast_to(table.T[None, :8], (rows // 8, 8, width))

    low, high = regroup(*tiles[:2]), regroup(*tiles[2:])
    for parity in range(2):
        joined = jnp.concatenate([low[parity], high[parity], sums], axis=1)
        out_ref[:, parity] = joined.astype(out_ref.dtype)


def cascade(parts, start):
    _, rows, width = parts.shape
    half = jax.ShapeDtypeStruct((rows, width), jnp.float32)
    out, final, scaled = call(
        cascade_kernel,
        "cascade",
        parts.size,
        2 * parts.size,
        out_shape=(jax.ShapeDtypeStruct((rows // 8, 2, 24, width), jnp.bfloat16), half, half),
    )(parts, start)
    return out.reshape(rows // 4, 24, width), final, scaled


def norm_kernel(got_ref, final_ref, scaled_ref, out_ref):
    planes = got_ref.shape[0]
    rows, width = final_ref.shape
    sums = got_ref[0, 16:24].astype(jnp.float32)
    for plane in range(1, planes):
        sums += got_ref[plane, 16:24].astype(jnp.float32)
    table = jnp.concatenate([sums, jnp.zeros((120, width), jnp.float32)], axis=0).T[:rows]
    lane = lax.broadcasted_iota(jnp.int32, table.shape, 1)
    square = jnp.sum(jnp.where(lane < 3, table, 0.0), axis=1, keepdims=True) / D
    mixed = jnp.sum(jnp.where(lane < 3, 0.0, table), axis=1, keepdims=True) / D
    inverse = lax.rsqrt(square + 1e-05)
    grad = inverse * (scaled_ref[...] - final_ref[...] * (inverse * inverse * mixed))

    shards = planes // 2
    spread = jnp.broadcast_to(grad[None], (shards, rows, width))
    pairs = got_ref[...].astype(jnp.float32).reshape(shards, 2, 24, width)
    for at in range(2):
        part = slice(8 * at, 8 * at + 8)
        for parity, tile in enumerate(regroup(pairs[:, 0, part], pairs[:, 1, part])):
            joined = jnp.concatenate([spread, tile], axis=1)
            out_ref[2 * at + parity] = joined.astype(out_ref.dtype)


def norm(got, final, scaled):
    rows, width = final.shape
    shards = got.shape[0] // 2
    out = call(
        norm_kernel,
        "norm_gradient",
        got.size,
        4 * got.size,
        out_shape=jax.ShapeDtypeStruct((4, shards, rows + 8, width), jnp.bfloat16),
    )(got, final, scaled)
    return out.reshape(4 * shards, rows + 8, width)


def gradient_kernel(kept_ref, full_ref, acts_ref, out_ref, section_ref, turned_ref, found_ref):
    cols, keep, blk, _ = out_ref.shape
    pairs, _, rows, width = full_ref.shape

    def tiles(at):
        even = full_ref[:, 0, at : at + 8].astype(jnp.float32)
        odd = full_ref[:, 1, at : at + 8].astype(jnp.float32)
        return [t.reshape(pairs * 8, width) for t in regroup(even, odd)]

    for two in range((rows - 8) // 8):
        for parity, tile in enumerate(tiles(8 * two)):
            at = (2 * two + parity) * pairs * 8
            turned_ref[:, at : at + pairs * 8] = tile.T.astype(turned_ref.dtype)
    for parity, tile in enumerate(tiles(rows - 8)):
        section_ref[:, parity * width : (parity + 1) * width] = tile.astype(section_ref.dtype)

    found_ref[...] = jnp.dot(
        turned_ref[...], acts_ref[...], preferred_element_type=jnp.float32
    ).astype(found_ref.dtype)
    for c in range(cols):
        for slot in range(keep):
            start = pl.multiple_of(kept_ref[c, slot] * blk, blk)
            out_ref[c, slot] = found_ref[c * blk : (c + 1) * blk, pl.ds(start, blk)].T


def gradient(own_kept, full, held, blk):
    tokens, units = held.shape
    devices, rows, width = full.shape
    cols, keep = own_kept.shape
    whole = pl.BlockSpec(memory_space=pltpu.VMEM)
    return call(
        gradient_kernel,
        "gradient_matmul",
        2 * tokens * units * width,
        2 * tokens * units,
        in_specs=[pl.BlockSpec(memory_space=pltpu.SMEM), whole, whole],
        out_specs=[whole, whole],
        scratch_shapes=[
            pltpu.VMEM((width, tokens), jnp.bfloat16),
            pltpu.VMEM((width, units), jnp.bfloat16),
        ],
        out_shape=(
            jax.ShapeDtypeStruct((cols, keep, blk, blk), jnp.bfloat16),
            jax.ShapeDtypeStruct((devices * HALF, 2 * width), jnp.bfloat16),
        ),
    )(own_kept, full.reshape(devices // 2, 2, rows, width), held)


def exchange(value, axes):
    return lax.all_to_all(value, axes, split_axis=0, concat_axis=0, tiled=True)


def body(hidden, residual_in, weights, kept, cotangent, norm_gain):
    ns, nz, nt = (lax.axis_size(a) for a in ALL)
    section, plane = lax.axis_index("section"), lax.axis_index("dp")
    acts = hidden[0]
    rows = acts.shape[0]
    blocks = weights[0, 0]
    cols, _, blk, _ = blocks.shape
    width = cols * blk
    hidden_blocks = acts.shape[1] // blk
    every = lax.all_gather(acts, "dp", axis=0, tiled=True)
    own_kept = lax.dynamic_slice_in_dim(kept[0, 0], plane * cols, cols, axis=0)
    hit = own_kept[None] == jnp.arange(hidden_blocks, dtype=own_kept.dtype)[:, None, None]
    dense = jnp.sum(
        jnp.where(hit[..., None, None], blocks[None].astype(jnp.float32), 0.0), axis=2
    ).astype(jnp.bfloat16)
    dense = dense.transpose(0, 2, 1, 3).reshape(hidden_blocks * blk, width)

    start = exchange(split(section, residual_in, cotangent, norm_gain), PLANE)
    start = exchange(join(start, nz), "dp")
    partial_out, held = forward(every, dense, rows, start)
    parts = exchange(partial_out, PLANE)
    sent, final, scaled = cascade(parts, start)
    spread = norm(exchange(sent, "dp"), final, scaled)
    grads, section_out = gradient(own_kept, exchange(spread, PLANE), held, blk)
    return (section_out[None], grads[None, None])


def solution(mesh):
    in_specs = (
        P("section", "dp", "tensor"),
        P("dp", "tensor"),
        P("section", "tensor", "dp", None, None, None),
        P("section", "tensor", None, None),
        P("dp", "tensor"),
        P("tensor"),
    )
    out_specs = (P("section", "dp", "tensor"), P("section", "tensor", "dp", None, None, None))
    return jax.shard_map(body, mesh=mesh, in_specs=in_specs, out_specs=out_specs, check_vma=False)
```

```python
import jax
import jax.numpy as jnp
from jax import lax
from jax.experimental import pallas as pl
from jax.experimental.pallas import tpu as pltpu
from jax.sharding import Mesh
from jax.sharding import PartitionSpec as P

D = 4096
TENSOR = ("x", "core")
CHIPS = ("section", "x")
HALF = 4


def regroup(even, odd):
    upper = lax.broadcasted_iota(jnp.int32, even.shape, even.ndim - 2) < HALF
    axis = even.ndim - 2
    first = jnp.where(upper, even, pltpu.roll(odd, HALF, axis))
    second = jnp.where(upper, pltpu.roll(even, HALF, axis), odd)
    return first, second


def call(kernel, name, flops, moved, vmem=16 << 20, **kwargs):
    return pl.pallas_call(
        kernel,
        compiler_params=pltpu.CompilerParams(vmem_limit_bytes=vmem),
        cost_estimate=pl.CostEstimate(flops=flops, bytes_accessed=moved, transcendentals=0),
        name=name,
        **kwargs,
    )


def split_kernel(section_ref, residual_ref, cot_ref, gain_ref, out_ref):
    rows, width = residual_ref.shape
    shape = (rows // 8, 8, width)
    scaled = cot_ref[...].astype(jnp.float32) * gain_ref[...]
    tiles = regroup(residual_ref[...].astype(jnp.float32).reshape(shape), scaled.reshape(shape))
    for half in range(2):
        for core in range(2):
            part = tiles[half][8 * core : 8 * core + 8].astype(out_ref.dtype)
            out_ref[half, :, core] = part


def split(section, residual, cotangent, gain):
    rows, width = residual.shape
    part = width // lax.axis_size("section")
    block = pl.BlockSpec((rows, part), lambda i, section: (0, section[0]))
    out = call(
        split_kernel,
        "split_rows",
        rows * part,
        6 * rows * part,
        grid_spec=pltpu.PrefetchScalarGridSpec(
            num_scalar_prefetch=1,
            grid=(1,),
            in_specs=[
                block,
                block,
                pl.BlockSpec((1, part), lambda i, section: (0, section[0])),
            ],
            out_specs=pl.BlockSpec((2, rows // 16, 2, 8, part), lambda i, section: (0,) * 5),
        ),
        out_shape=jax.ShapeDtypeStruct((2, rows // 16, 2, 8, part), jnp.bfloat16),
    )(section.astype(jnp.int32).reshape(1), residual, cotangent, gain.reshape(1, width))
    return out.reshape(rows // 4, 8, part)


def join_kernel(got_ref, out_ref):
    part = got_ref.shape[2]
    shards = out_ref.shape[0] // 2
    for half in range(2):
        for shard in range(shards):
            for side in range(2):
                tile = got_ref[(2 * half + side) * shards + shard]
                out_ref[2 * shard + half, :, side * part : (side + 1) * part] = tile


def join(got, planes):
    _, rows, part = got.shape
    shape = (planes, rows, 2 * part)
    return call(
        join_kernel,
        "join_columns",
        got.size,
        4 * got.size,
        grid=(1,),
        in_specs=[pl.BlockSpec(got.shape, lambda i: (0, 0, 0))],
        out_specs=pl.BlockSpec(shape, lambda i: (0, 0, 0)),
        out_shape=jax.ShapeDtypeStruct(shape, got.dtype),
    )(got)


def partial_sums(core, acts_ref, dense_ref, out_ref, added_ref=None):
    groups, _, rows, units = acts_ref.shape
    width = dense_ref.shape[1]
    for step in range(groups // 8):
        acts = acts_ref[8 * step : 8 * step + 8, core].reshape(8 * rows, units)
        found = jnp.dot(acts, dense_ref[...], preferred_element_type=jnp.float32)
        found = found.reshape(8, rows // 8, 8, width)
        pairs = [regroup(found[2 * q], found[2 * q + 1]) for q in range(4)]
        at = slice(32 * step, 32 * step + 32)
        for half in range(2):
            joined = jnp.concatenate([pair[half] for pair in pairs], axis=1)
            if added_ref is not None:
                joined += added_ref[half, :, at].astype(jnp.float32)
            out_ref[half, :, at] = joined.astype(out_ref.dtype)


def other_kernel(core_ref, acts_ref, dense_ref, after_ref, out_ref, held_ref):
    for group in range(acts_ref.shape[0]):
        held_ref[group] = acts_ref[group]
    partial_sums(1 - core_ref[0], acts_ref, dense_ref, out_ref)


def own_kernel(core_ref, held_ref, dense_ref, added_ref, out_ref):
    partial_sums(core_ref[0], held_ref, dense_ref, out_ref, added_ref)


def forward(core, every, dense, rows, after):
    tokens, units = every.shape
    width = dense.shape[1]
    groups = tokens // rows
    shape = (groups, 2, rows // 2, units)
    out = jax.ShapeDtypeStruct((2, rows // 16, HALF * groups, width), jnp.bfloat16)
    whole = pl.BlockSpec(memory_space=pltpu.VMEM)
    scalar = pl.BlockSpec(memory_space=pltpu.SMEM)
    sent, held = call(
        other_kernel,
        "other_core_matmul",
        tokens * units * width,
        2 * tokens * units,
        in_specs=[scalar, whole, whole, pl.BlockSpec(memory_space=pl.ANY)],
        out_specs=[whole, whole],
        out_shape=(out, pltpu.VMEM(shape, every.dtype)),
    )(core, every.reshape(shape), dense, after)
    got = lax.ppermute(sent, "core", [(0, 1), (1, 0)])
    both = call(
        own_kernel,
        "own_core_matmul",
        tokens * units * width,
        tokens * units,
        in_specs=[scalar, whole, whole, whole],
        out_specs=whole,
        out_shape=out,
    )(core, held, dense, got)
    return both.reshape(rows // 8, HALF * groups, width), held


def cascade_kernel(parts_ref, start_ref, out_ref, final_ref, scaled_ref):
    rows, width = final_ref.shape
    shards = parts_ref.shape[0] // 4
    start = start_ref[...].astype(jnp.float32).reshape(rows // 8, 2, 8, width)
    current, scaled = (t.reshape(rows, width) for t in regroup(start[:, 0], start[:, 1]))
    tiles = []
    for section in range(4):
        contrib = parts_ref[section * shards].astype(jnp.float32)
        for shard in range(1, shards):
            contrib += parts_ref[section * shards + shard].astype(jnp.float32)
        current = (current + contrib).astype(jnp.bfloat16).astype(jnp.float32)
        tiles.append(current.reshape(rows // 8, 8, width))
    final_ref[...] = current
    scaled_ref[...] = scaled

    lane = lax.broadcasted_iota(jnp.int32, (rows, 128), 1)
    table = jnp.zeros((rows, 128), jnp.float32)
    for at, factor in enumerate((current, scaled)):
        left = jnp.sum(factor * current, axis=1, keepdims=True)
        for term in range(3):
            head = left.astype(jnp.bfloat16).astype(jnp.float32)
            table = jnp.where(lane == 3 * at + term, head, table)
            left = left - head
    table = jnp.concatenate([table, jnp.zeros((128 - rows, 128), jnp.float32)], axis=0)
    sums = jnp.broadcast_to(table.T[None, :8], (rows // 8, 8, 128))

    low, high = regroup(*tiles[:2]), regroup(*tiles[2:])
    for parity in range(2):
        sides = [
            part[parity][:, :, at : at + 128] for at in range(0, width, 128) for part in (low, high)
        ]
        out_ref[:, parity] = jnp.concatenate(sides + [sums], axis=1).astype(out_ref.dtype)


def cascade(parts, start):
    _, rows, width = parts.shape
    half = jax.ShapeDtypeStruct((rows, width), jnp.float32)
    out, final, scaled = call(
        cascade_kernel,
        "cascade",
        parts.size,
        2 * parts.size,
        out_shape=(jax.ShapeDtypeStruct((rows // 8, 2, 40, 128), jnp.bfloat16), half, half),
    )(parts, start)
    return out.reshape(rows // 4, 40, 128), final, scaled


def norm_kernel(core_ref, got_ref, final_ref, scaled_ref, out_ref):
    planes = got_ref.shape[0]
    rows, width = final_ref.shape
    sums = got_ref[0, 32:40].astype(jnp.float32)
    for plane in range(1, planes):
        sums += got_ref[plane, 32:40].astype(jnp.float32)
    table = jnp.concatenate([sums, jnp.zeros((120, 128), jnp.float32)], axis=0).T[:rows]
    lane = lax.broadcasted_iota(jnp.int32, table.shape, 1)
    square = jnp.sum(jnp.where(lane < 3, table, 0.0), axis=1, keepdims=True) / D
    mixed = jnp.sum(jnp.where(lane < 3, 0.0, table), axis=1, keepdims=True) / D
    inverse = lax.rsqrt(square + 1e-05)
    grad = inverse * (scaled_ref[...] - final_ref[...] * (inverse * inverse * mixed))

    shards = planes // 2
    first = core_ref[0] == 0
    spread = jnp.broadcast_to(grad[None], (shards // 2, rows, width))
    pairs = got_ref[...].astype(jnp.float32).reshape(shards, 2, 40, 128)
    for at in range(2):
        even, odd = (
            jnp.concatenate([pairs[:, q, row : row + 8] for row in (8 * at, 8 * at + 16)], axis=2)
            for q in range(2)
        )
        for parity, tile in enumerate(regroup(even, odd)):
            tile = tile.reshape(shards // 2, 2, 8, width)
            same = jnp.where(first, tile[:, 0], tile[:, 1])
            other = jnp.where(first, tile[:, 1], tile[:, 0])
            joined = jnp.concatenate([spread, same, other], axis=1)
            out_ref[2 * at + parity] = joined.astype(out_ref.dtype)


def norm(core, got, final, scaled):
    rows, width = final.shape
    chips = got.shape[0] // 4
    whole = pl.BlockSpec(memory_space=pltpu.VMEM)
    out = call(
        norm_kernel,
        "norm_gradient",
        got.size,
        4 * got.size,
        in_specs=[pl.BlockSpec(memory_space=pltpu.SMEM), whole, whole, whole],
        out_specs=whole,
        out_shape=jax.ShapeDtypeStruct((4, chips, rows + 16, width), jnp.bfloat16),
    )(core, got, final, scaled)
    return out.reshape(4 * chips, rows + 16, width)


def products(core, full_ref, acts_ref, turned_ref, section_at):
    groups, _, rows, units = acts_ref.shape
    _, tiles, _, width = full_ref.shape

    def regrouped(at):
        even = full_ref[0, :, at : at + 8].astype(jnp.float32)
        odd = full_ref[1, :, at : at + 8].astype(jnp.float32)
        return [t.reshape(8 * tiles, width) for t in regroup(even, odd)]

    for two in range(groups // 2):
        pair = jnp.concatenate(regrouped(8 * two), axis=0)
        at = 2 * two * rows
        turned_ref[:, at : at + 2 * rows] = pair.T.astype(turned_ref.dtype)
    found = None
    for step in range(2):
        part = groups // 2
        acts = acts_ref[step * part : (step + 1) * part, core].reshape(part * rows, units)
        term = jnp.dot(
            turned_ref[:, step * part * rows : (step + 1) * part * rows],
            acts,
            preferred_element_type=jnp.float32,
        )
        found = term if found is None else found + term
    return found, jnp.concatenate(regrouped(section_at), axis=1)


def near_kernel(core_ref, full_ref, acts_ref, found_ref, section_ref, turned_ref):
    rows = full_ref.shape[2]
    found, section = products(core_ref[0], full_ref, acts_ref, turned_ref, rows - 16)
    found_ref[...] = found
    section_ref[...] = section.astype(section_ref.dtype)


def far_kernel(
    core_ref,
    kept_ref,
    full_ref,
    acts_ref,
    near_ref,
    near_section_ref,
    out_ref,
    section_ref,
    turned_ref,
    found_ref,
):
    cols, keep, blk, _ = out_ref.shape
    core, rows = core_ref[0], full_ref.shape[2]
    found, section = products(1 - core, full_ref, acts_ref, turned_ref, rows - 8)
    half = section_ref.shape[0] // 2
    section_ref[pl.ds(pl.multiple_of(core * half, half), half)] = near_section_ref[...]
    section_ref[pl.ds(pl.multiple_of((1 - core) * half, half), half)] = section.astype(
        section_ref.dtype
    )
    found_ref[...] = (near_ref[...] + found).astype(found_ref.dtype)
    for c in range(cols):
        for slot in range(keep):
            start = pl.multiple_of(kept_ref[c, slot] * blk, blk)
            out_ref[c, slot] = found_ref[c * blk : (c + 1) * blk, pl.ds(start, blk)].T


def gradient(core, own_kept, full, held, blk):
    groups, _, rows, units = held.shape
    chips, _, width = full.shape
    cols, keep = own_kept.shape
    full = full.reshape(2, chips // 2, *full.shape[1:])
    whole = pl.BlockSpec(memory_space=pltpu.VMEM)
    scalar = pl.BlockSpec(memory_space=pltpu.SMEM)
    turned = pltpu.VMEM((width, groups * rows), jnp.bfloat16)
    flops = 2 * groups * rows * units * width
    other = lax.ppermute(full, "core", [(0, 1), (1, 0)])
    found, section = call(
        near_kernel,
        "own_core_gradient",
        flops,
        held.size,
        in_specs=[scalar, whole, whole],
        out_specs=[whole, whole],
        scratch_shapes=[turned],
        out_shape=(
            jax.ShapeDtypeStruct((width, units), jnp.float32),
            jax.ShapeDtypeStruct((rows, 2 * width), jnp.bfloat16),
        ),
    )(core, full, held)
    return call(
        far_kernel,
        "other_core_gradient",
        flops,
        held.size,
        in_specs=[scalar, scalar] + [whole] * 4,
        out_specs=[whole, whole],
        scratch_shapes=[turned, pltpu.VMEM((width, units), jnp.bfloat16)],
        out_shape=(
            jax.ShapeDtypeStruct((cols, keep, blk, blk), jnp.bfloat16),
            jax.ShapeDtypeStruct((2 * rows, 2 * width), jnp.bfloat16),
        ),
    )(core, own_kept, other, held, found, section)


def exchange(value, axes):
    return lax.all_to_all(value, axes, split_axis=0, concat_axis=0, tiled=True)


def body(hidden, residual_in, weights, kept, cotangent, norm_gain):
    nz = lax.axis_size("dp")
    core = lax.axis_index("core").astype(jnp.int32).reshape(1)
    section, plane = lax.axis_index("section"), lax.axis_index("dp")
    acts = hidden[0]
    rows = acts.shape[0]
    blocks = weights[0, 0]
    cols, _, blk, _ = blocks.shape
    width = cols * blk
    hidden_blocks = acts.shape[1] // blk
    every = lax.all_gather(acts, "dp", axis=0, tiled=True)
    own_kept = lax.dynamic_slice_in_dim(kept[0, 0], plane * cols, cols, axis=0)
    hit = own_kept[None] == jnp.arange(hidden_blocks, dtype=own_kept.dtype)[:, None, None]
    dense = jnp.sum(
        jnp.where(hit[..., None, None], blocks[None].astype(jnp.float32), 0.0), axis=2
    ).astype(jnp.bfloat16)
    dense = dense.transpose(0, 2, 1, 3).reshape(hidden_blocks * blk, width)

    start = exchange(split(section, residual_in, cotangent, norm_gain), ("section",) + TENSOR)
    start = exchange(join(start, nz), "dp")
    partial_out, held = forward(core, every, dense, rows, start)
    sent, final, scaled = cascade(exchange(partial_out, CHIPS), start)
    spread = norm(core, exchange(sent, "dp"), final, scaled)
    grads, section_out = gradient(core, own_kept, exchange(spread, CHIPS), held, blk)
    return (section_out[None], grads[None, None])


def solution(mesh):
    sizes = mesh.shape
    shape = (sizes["section"], sizes["dp"], sizes["tensor"] // 2, 2)
    chips = Mesh(mesh.devices.reshape(shape), ("section", "dp") + TENSOR)
    in_specs = (
        P("section", "dp", TENSOR),
        P("dp", TENSOR),
        P("section", TENSOR, "dp", None, None, None),
        P("section", TENSOR, None, None),
        P("dp", TENSOR),
        P(TENSOR),
    )
    out_specs = (P("section", "dp", TENSOR), P("section", TENSOR, "dp", None, None, None))
    return jax.shard_map(body, mesh=chips, in_specs=in_specs, out_specs=out_specs, check_vma=False)
```

```python
import jax
import jax.numpy as jnp
from jax import lax
from jax.experimental import pallas as pl
from jax.experimental.pallas import tpu as pltpu
from jax.sharding import Mesh
from jax.sharding import PartitionSpec as P

D = 4096
TENSOR = ("x", "core")
CHIPS = ("section", "x")
HALF = 4


def regroup(even, odd):
    upper = lax.broadcasted_iota(jnp.int32, even.shape, even.ndim - 2) < HALF
    axis = even.ndim - 2
    first = jnp.where(upper, even, pltpu.roll(odd, HALF, axis))
    second = jnp.where(upper, pltpu.roll(even, HALF, axis), odd)
    return first, second


def call(kernel, name, flops, moved, vmem=16 << 20, **kwargs):
    return pl.pallas_call(
        kernel,
        compiler_params=pltpu.CompilerParams(vmem_limit_bytes=vmem),
        cost_estimate=pl.CostEstimate(flops=flops, bytes_accessed=moved, transcendentals=0),
        name=name,
        **kwargs,
    )


def split_kernel(section_ref, residual_ref, cot_ref, gain_ref, out_ref):
    rows, width = residual_ref.shape
    shape = (rows // 8, 8, width)
    scaled = cot_ref[...].astype(jnp.float32) * gain_ref[...]
    tiles = regroup(residual_ref[...].astype(jnp.float32).reshape(shape), scaled.reshape(shape))
    for half in range(2):
        for core in range(2):
            part = tiles[half][8 * core : 8 * core + 8].astype(out_ref.dtype)
            out_ref[half, :, core] = part


def split(section, residual, cotangent, gain):
    rows, width = residual.shape
    part = width // lax.axis_size("section")
    block = pl.BlockSpec((rows, part), lambda i, section: (0, section[0]))
    out = call(
        split_kernel,
        "split_rows",
        rows * part,
        6 * rows * part,
        grid_spec=pltpu.PrefetchScalarGridSpec(
            num_scalar_prefetch=1,
            grid=(1,),
            in_specs=[
                block,
                block,
                pl.BlockSpec((1, part), lambda i, section: (0, section[0])),
            ],
            out_specs=pl.BlockSpec((2, rows // 16, 2, 8, part), lambda i, section: (0,) * 5),
        ),
        out_shape=jax.ShapeDtypeStruct((2, rows // 16, 2, 8, part), jnp.bfloat16),
    )(section.astype(jnp.int32).reshape(1), residual, cotangent, gain.reshape(1, width))
    return out.reshape(rows // 4, 8, part)


def join_kernel(got_ref, left_ref, right_ref):
    shards = left_ref.shape[0] // 2
    for half in range(2):
        for shard in range(shards):
            for side, out_ref in enumerate((left_ref, right_ref)):
                out_ref[2 * shard + half] = got_ref[(2 * half + side) * shards + shard]


def join(got, planes):
    _, rows, part = got.shape
    shape = (planes, rows, part)
    return call(
        join_kernel,
        "join_columns",
        got.size,
        4 * got.size,
        grid=(1,),
        in_specs=[pl.BlockSpec(got.shape, lambda i: (0, 0, 0))],
        out_specs=[pl.BlockSpec(shape, lambda i: (0, 0, 0))] * 2,
        out_shape=[jax.ShapeDtypeStruct(shape, got.dtype)] * 2,
    )(got)


def partial_sums(core, acts_ref, dense_ref, out_ref):
    groups, _, rows, units = acts_ref.shape
    width = dense_ref.shape[1]
    for step in range(groups // 8):
        acts = acts_ref[8 * step : 8 * step + 8, core].reshape(8 * rows, units)
        found = jnp.dot(acts, dense_ref[...], preferred_element_type=jnp.float32)
        found = found.reshape(8, rows // 8, 8, width)
        pairs = [regroup(found[2 * q], found[2 * q + 1]) for q in range(4)]
        at = slice(32 * step, 32 * step + 32)
        for half in range(2):
            joined = jnp.concatenate([pair[half] for pair in pairs], axis=1)
            out_ref[half, :, at] = joined.astype(out_ref.dtype)


def other_kernel(core_ref, acts_ref, dense_ref, left_ref, right_ref, out_ref, held_ref):
    for group in range(acts_ref.shape[0]):
        held_ref[group] = acts_ref[group]
    partial_sums(1 - core_ref[0], acts_ref, dense_ref, out_ref)


def own_kernel(core_ref, held_ref, dense_ref, out_ref):
    partial_sums(core_ref[0], held_ref, dense_ref, out_ref)


def add_kernel(own_ref, got_ref, out_ref):
    out_ref[...] = (own_ref[...] + got_ref[...].astype(jnp.float32)).astype(out_ref.dtype)


def forward(core, every, dense, rows, after):
    tokens, units = every.shape
    width = dense.shape[1]
    groups = tokens // rows
    shape = (groups, 2, rows // 2, units)
    out = jax.ShapeDtypeStruct((2, rows // 16, HALF * groups, width), jnp.bfloat16)
    whole = pl.BlockSpec(memory_space=pltpu.VMEM)
    scalar = pl.BlockSpec(memory_space=pltpu.SMEM)
    sent, held = call(
        other_kernel,
        "other_core_matmul",
        tokens * units * width,
        2 * tokens * units,
        in_specs=[scalar, whole, whole] + [pl.BlockSpec(memory_space=pl.ANY)] * 2,
        out_specs=[whole, whole],
        out_shape=(out, pltpu.VMEM(shape, every.dtype)),
    )(core, every.reshape(shape), dense, *after)
    got = lax.ppermute(sent, "core", [(0, 1), (1, 0)])
    own = call(
        own_kernel,
        "own_core_matmul",
        tokens * units * width,
        tokens * units,
        in_specs=[scalar, whole, whole],
        out_specs=whole,
        out_shape=jax.ShapeDtypeStruct(out.shape, jnp.float32),
    )(core, held, dense)
    both = call(
        add_kernel,
        "add_cores",
        out.size,
        8 * out.size,
        in_specs=[whole] * 2,
        out_specs=whole,
        out_shape=out,
    )(own, got)
    return both.reshape(rows // 8, HALF * groups, width), held


def cascade_kernel(parts_ref, left_ref, right_ref, out_ref, final_ref, scaled_ref):
    rows, width = final_ref.shape
    shards = parts_ref.shape[0] // 4
    start = jnp.concatenate([left_ref[...], right_ref[...]], axis=2).astype(jnp.float32)
    start = start.reshape(rows // 8, 2, 8, width)
    current, scaled = (t.reshape(rows, width) for t in regroup(start[:, 0], start[:, 1]))
    tiles = []
    for section in range(4):
        contrib = parts_ref[section * shards].astype(jnp.float32)
        for shard in range(1, shards):
            contrib += parts_ref[section * shards + shard].astype(jnp.float32)
        current = (current + contrib).astype(jnp.bfloat16).astype(jnp.float32)
        tiles.append(current.reshape(rows // 8, 8, width))
    final_ref[...] = current
    scaled_ref[...] = scaled

    lane = lax.broadcasted_iota(jnp.int32, (rows, 128), 1)
    table = jnp.zeros((rows, 128), jnp.float32)
    for at, factor in enumerate((current, scaled)):
        left = jnp.sum(factor * current, axis=1, keepdims=True)
        for term in range(3):
            head = left.astype(jnp.bfloat16).astype(jnp.float32)
            table = jnp.where(lane == 3 * at + term, head, table)
            left = left - head
    table = jnp.concatenate([table, jnp.zeros((128 - rows, 128), jnp.float32)], axis=0)
    sums = jnp.broadcast_to(table.T[None, :8], (rows // 8, 8, 128))

    low, high = regroup(*tiles[:2]), regroup(*tiles[2:])
    for parity in range(2):
        sides = [
            part[parity][:, :, at : at + 128] for at in range(0, width, 128) for part in (low, high)
        ]
        out_ref[:, parity] = jnp.concatenate(sides + [sums], axis=1).astype(out_ref.dtype)


def cascade(parts, start):
    _, rows, width = parts.shape
    half = jax.ShapeDtypeStruct((rows, width), jnp.float32)
    out, final, scaled = call(
        cascade_kernel,
        "cascade",
        parts.size,
        2 * parts.size,
        out_shape=(jax.ShapeDtypeStruct((rows // 8, 2, 40, 128), jnp.bfloat16), half, half),
    )(parts, *start)
    return out.reshape(rows // 4, 40, 128), final, scaled


def norm_kernel(core_ref, got_ref, final_ref, scaled_ref, out_ref):
    planes = got_ref.shape[0]
    rows, width = final_ref.shape
    sums = got_ref[0, 32:40].astype(jnp.float32)
    for plane in range(1, planes):
        sums += got_ref[plane, 32:40].astype(jnp.float32)
    table = jnp.concatenate([sums, jnp.zeros((120, 128), jnp.float32)], axis=0).T[:rows]
    lane = lax.broadcasted_iota(jnp.int32, table.shape, 1)
    square = jnp.sum(jnp.where(lane < 3, table, 0.0), axis=1, keepdims=True) / D
    mixed = jnp.sum(jnp.where(lane < 3, 0.0, table), axis=1, keepdims=True) / D
    inverse = lax.rsqrt(square + 1e-05)
    grad = inverse * (scaled_ref[...] - final_ref[...] * (inverse * inverse * mixed))

    shards = planes // 2
    first = core_ref[0] == 0
    spread = jnp.broadcast_to(grad[None], (shards // 2, rows, width))
    pairs = got_ref[...].astype(jnp.float32).reshape(shards, 2, 40, 128)
    for at in range(2):
        even, odd = (
            jnp.concatenate([pairs[:, q, row : row + 8] for row in (8 * at, 8 * at + 16)], axis=2)
            for q in range(2)
        )
        for parity, tile in enumerate(regroup(even, odd)):
            tile = tile.reshape(shards // 2, 2, 8, width)
            same = jnp.where(first, tile[:, 0], tile[:, 1])
            other = jnp.where(first, tile[:, 1], tile[:, 0])
            joined = jnp.concatenate([spread, same, other], axis=1)
            out_ref[2 * at + parity] = joined.astype(out_ref.dtype)


def norm(core, got, final, scaled):
    rows, width = final.shape
    chips = got.shape[0] // 4
    whole = pl.BlockSpec(memory_space=pltpu.VMEM)
    out = call(
        norm_kernel,
        "norm_gradient",
        got.size,
        4 * got.size,
        in_specs=[pl.BlockSpec(memory_space=pltpu.SMEM), whole, whole, whole],
        out_specs=whole,
        out_shape=jax.ShapeDtypeStruct((4, chips, rows + 16, width), jnp.bfloat16),
    )(core, got, final, scaled)
    return out.reshape(4 * chips, rows + 16, width)


def products(core, full_ref, acts_ref, turned_ref, section_at):
    groups, _, rows, units = acts_ref.shape
    _, tiles, _, width = full_ref.shape

    def regrouped(at):
        even = full_ref[0, :, at : at + 8].astype(jnp.float32)
        odd = full_ref[1, :, at : at + 8].astype(jnp.float32)
        return [t.reshape(8 * tiles, width) for t in regroup(even, odd)]

    for two in range(groups // 2):
        pair = jnp.concatenate(regrouped(8 * two), axis=0)
        at = 2 * two * rows
        turned_ref[:, at : at + 2 * rows] = pair.T.astype(turned_ref.dtype)
    found = None
    for step in range(2):
        part = groups // 2
        acts = acts_ref[step * part : (step + 1) * part, core].reshape(part * rows, units)
        term = jnp.dot(
            turned_ref[:, step * part * rows : (step + 1) * part * rows],
            acts,
            preferred_element_type=jnp.float32,
        )
        found = term if found is None else found + term
    return found, jnp.concatenate(regrouped(section_at), axis=1)


def near_kernel(core_ref, full_ref, acts_ref, found_ref, section_ref, turned_ref):
    rows = full_ref.shape[2]
    found, section = products(core_ref[0], full_ref, acts_ref, turned_ref, rows - 16)
    found_ref[...] = found
    section_ref[...] = section.astype(section_ref.dtype)


def far_kernel(
    core_ref,
    kept_ref,
    full_ref,
    acts_ref,
    near_ref,
    near_section_ref,
    out_ref,
    section_ref,
    turned_ref,
    found_ref,
):
    cols, keep, blk, _ = out_ref.shape
    core, rows = core_ref[0], full_ref.shape[2]
    found, section = products(1 - core, full_ref, acts_ref, turned_ref, rows - 8)
    half = section_ref.shape[0] // 2
    section_ref[pl.ds(pl.multiple_of(core * half, half), half)] = near_section_ref[...]
    section_ref[pl.ds(pl.multiple_of((1 - core) * half, half), half)] = section.astype(
        section_ref.dtype
    )
    found_ref[...] = (near_ref[...] + found).astype(found_ref.dtype)
    for c in range(cols):
        for slot in range(keep):
            start = pl.multiple_of(kept_ref[c, slot] * blk, blk)
            out_ref[c, slot] = found_ref[c * blk : (c + 1) * blk, pl.ds(start, blk)].T


def gradient(core, own_kept, full, held, blk):
    groups, _, rows, units = held.shape
    chips, _, width = full.shape
    cols, keep = own_kept.shape
    full = full.reshape(2, chips // 2, *full.shape[1:])
    whole = pl.BlockSpec(memory_space=pltpu.VMEM)
    scalar = pl.BlockSpec(memory_space=pltpu.SMEM)
    turned = pltpu.VMEM((width, groups * rows), jnp.bfloat16)
    flops = 2 * groups * rows * units * width
    other = lax.ppermute(full, "core", [(0, 1), (1, 0)])
    found, section = call(
        near_kernel,
        "own_core_gradient",
        flops,
        held.size,
        in_specs=[scalar, whole, whole],
        out_specs=[whole, whole],
        scratch_shapes=[turned],
        out_shape=(
            jax.ShapeDtypeStruct((width, units), jnp.float32),
            jax.ShapeDtypeStruct((rows, 2 * width), jnp.bfloat16),
        ),
    )(core, full, held)
    return call(
        far_kernel,
        "other_core_gradient",
        flops,
        held.size,
        in_specs=[scalar, scalar] + [whole] * 4,
        out_specs=[whole, whole],
        scratch_shapes=[turned, pltpu.VMEM((width, units), jnp.bfloat16)],
        out_shape=(
            jax.ShapeDtypeStruct((cols, keep, blk, blk), jnp.bfloat16),
            jax.ShapeDtypeStruct((2 * rows, 2 * width), jnp.bfloat16),
        ),
    )(core, own_kept, other, held, found, section)


def exchange(value, axes):
    return lax.all_to_all(value, axes, split_axis=0, concat_axis=0, tiled=True)


def body(hidden, residual_in, weights, kept, cotangent, norm_gain):
    nz = lax.axis_size("dp")
    core = lax.axis_index("core").astype(jnp.int32).reshape(1)
    section, plane = lax.axis_index("section"), lax.axis_index("dp")
    acts = hidden[0]
    rows = acts.shape[0]
    blocks = weights[0, 0]
    cols, _, blk, _ = blocks.shape
    width = cols * blk
    hidden_blocks = acts.shape[1] // blk
    every = lax.all_gather(acts, "dp", axis=0, tiled=True)
    own_kept = lax.dynamic_slice_in_dim(kept[0, 0], plane * cols, cols, axis=0)
    hit = own_kept[None] == jnp.arange(hidden_blocks, dtype=own_kept.dtype)[:, None, None]
    dense = jnp.sum(
        jnp.where(hit[..., None, None], blocks[None].astype(jnp.float32), 0.0), axis=2
    ).astype(jnp.bfloat16)
    dense = dense.transpose(0, 2, 1, 3).reshape(hidden_blocks * blk, width)

    start = exchange(split(section, residual_in, cotangent, norm_gain), ("section",) + TENSOR)
    start = [exchange(side, "dp") for side in join(start, nz)]
    partial_out, held = forward(core, every, dense, rows, start)
    sent, final, scaled = cascade(exchange(partial_out, CHIPS), start)
    spread = norm(core, exchange(sent, "dp"), final, scaled)
    grads, section_out = gradient(core, own_kept, exchange(spread, CHIPS), held, blk)
    return (section_out[None], grads[None, None])


def solution(mesh):
    sizes = mesh.shape
    shape = (sizes["section"], sizes["dp"], sizes["tensor"] // 2, 2)
    chips = Mesh(mesh.devices.reshape(shape), ("section", "dp") + TENSOR)
    in_specs = (
        P("section", "dp", TENSOR),
        P("dp", TENSOR),
        P("section", TENSOR, "dp", None, None, None),
        P("section", TENSOR, None, None),
        P("dp", TENSOR),
        P(TENSOR),
    )
    out_specs = (P("section", "dp", TENSOR), P("section", TENSOR, "dp", None, None, None))
    return jax.shard_map(body, mesh=chips, in_specs=in_specs, out_specs=out_specs, check_vma=False)
```

```python
import jax
import jax.numpy as jnp
from jax import lax
from jax.experimental import pallas as pl
from jax.experimental.pallas import tpu as pltpu
from jax.sharding import Mesh
from jax.sharding import PartitionSpec as P

D = 4096
TENSOR = ("x", "core")
CHIPS = ("section", "x")
HALF = 4


def regroup(even, odd):
    upper = lax.broadcasted_iota(jnp.int32, even.shape, even.ndim - 2) < HALF
    axis = even.ndim - 2
    first = jnp.where(upper, even, pltpu.roll(odd, HALF, axis))
    second = jnp.where(upper, pltpu.roll(even, HALF, axis), odd)
    return first, second


def call(kernel, name, flops, moved, vmem=16 << 20, **kwargs):
    return pl.pallas_call(
        kernel,
        compiler_params=pltpu.CompilerParams(vmem_limit_bytes=vmem),
        cost_estimate=pl.CostEstimate(flops=flops, bytes_accessed=moved, transcendentals=0),
        name=name,
        **kwargs,
    )


def split_kernel(section_ref, residual_ref, cot_ref, gain_ref, out_ref):
    rows, width = residual_ref.shape
    shape = (rows // 8, 8, width)
    scaled = cot_ref[...].astype(jnp.float32) * gain_ref[...]
    tiles = regroup(residual_ref[...].astype(jnp.float32).reshape(shape), scaled.reshape(shape))
    for half in range(2):
        out_ref[half] = tiles[half].astype(out_ref.dtype)


def split(section, residual, cotangent, gain):
    rows, width = residual.shape
    shape = (rows // 2, width // 2)
    block = pl.BlockSpec(shape, lambda i, s: (s[0] // 2, lax.rem(s[0], 2)))
    out = call(
        split_kernel,
        "split_rows",
        rows * width,
        2 * rows * width,
        grid_spec=pltpu.PrefetchScalarGridSpec(
            num_scalar_prefetch=1,
            grid=(1,),
            in_specs=[
                block,
                block,
                pl.BlockSpec((1, shape[1]), lambda i, s: (0, lax.rem(s[0], 2))),
            ],
            out_specs=pl.BlockSpec((2, rows // 16, 8, shape[1]), lambda i, s: (0,) * 4),
        ),
        out_shape=jax.ShapeDtypeStruct((2, rows // 16, 8, shape[1]), jnp.bfloat16),
    )(section.astype(jnp.int32).reshape(1), residual, cotangent, gain.reshape(1, width))
    return out.reshape(rows // 8, 8, shape[1])


def to_columns(ns, nz, nx):
    pairs = []
    for s in range(ns):
        for z in range(nz):
            for t in range(2 * nx):
                source = (s * nz + z) * 2 * nx + t
                plane = 2 * t + s % 2
                pairs.append((source, ((z // nx * nz + plane) * nx + z % nx) * 2 + s // 2))
    return pairs


def partial_sums(core, acts_ref, dense_ref, out_ref):
    groups, _, rows, units = acts_ref.shape
    width = dense_ref.shape[1]
    for step in range(groups // 8):
        acts = acts_ref[8 * step : 8 * step + 8, core].reshape(8 * rows, units)
        found = jnp.dot(acts, dense_ref[...], preferred_element_type=jnp.float32)
        found = found.reshape(8, rows // 8, 8, width)
        pairs = [regroup(found[2 * q], found[2 * q + 1]) for q in range(4)]
        at = slice(32 * step, 32 * step + 32)
        for half in range(2):
            joined = jnp.concatenate([pair[half] for pair in pairs], axis=1)
            out_ref[half, :, at] = joined.astype(out_ref.dtype)


def other_kernel(core_ref, acts_ref, dense_ref, after_ref, out_ref, held_ref):
    for group in range(acts_ref.shape[0]):
        held_ref[group] = acts_ref[group]
    partial_sums(1 - core_ref[0], acts_ref, dense_ref, out_ref)


def own_kernel(core_ref, held_ref, dense_ref, out_ref):
    partial_sums(core_ref[0], held_ref, dense_ref, out_ref)


def add_kernel(own_ref, got_ref, out_ref):
    out_ref[...] = (own_ref[...] + got_ref[...].astype(jnp.float32)).astype(out_ref.dtype)


def forward(core, every, dense, rows, after):
    tokens, units = every.shape
    width = dense.shape[1]
    groups = tokens // rows
    shape = (groups, 2, rows // 2, units)
    out = jax.ShapeDtypeStruct((2, rows // 16, HALF * groups, width), jnp.bfloat16)
    whole = pl.BlockSpec(memory_space=pltpu.VMEM)
    scalar = pl.BlockSpec(memory_space=pltpu.SMEM)
    sent, held = call(
        other_kernel,
        "other_core_matmul",
        tokens * units * width,
        2 * tokens * units,
        in_specs=[scalar, whole, whole, pl.BlockSpec(memory_space=pl.ANY)],
        out_specs=[whole, whole],
        out_shape=(out, pltpu.VMEM(shape, every.dtype)),
    )(core, every.reshape(shape), dense, after)
    got = lax.ppermute(sent, "core", [(0, 1), (1, 0)])
    own = call(
        own_kernel,
        "own_core_matmul",
        tokens * units * width,
        tokens * units,
        in_specs=[scalar, whole, whole],
        out_specs=whole,
        out_shape=jax.ShapeDtypeStruct(out.shape, jnp.float32),
    )(core, held, dense)
    both = call(
        add_kernel,
        "add_cores",
        out.size,
        8 * out.size,
        in_specs=[whole] * 2,
        out_specs=whole,
        out_shape=out,
    )(own, got)
    return both.reshape(rows // 8, HALF * groups, width), held


def cascade_kernel(parts_ref, start_ref, out_ref, final_ref, scaled_ref):
    rows, width = final_ref.shape
    shards = parts_ref.shape[0] // 4
    start = start_ref[...].astype(jnp.float32).reshape(rows // 8, 2, 8, width)
    current, scaled = (t.reshape(rows, width) for t in regroup(start[:, 0], start[:, 1]))
    tiles = []
    for section in range(4):
        contrib = parts_ref[section * shards].astype(jnp.float32)
        for shard in range(1, shards):
            contrib += parts_ref[section * shards + shard].astype(jnp.float32)
        current = (current + contrib).astype(jnp.bfloat16).astype(jnp.float32)
        tiles.append(current.reshape(rows // 8, 8, width))
    final_ref[...] = current
    scaled_ref[...] = scaled

    lane = lax.broadcasted_iota(jnp.int32, (rows, 128), 1)
    table = jnp.zeros((rows, 128), jnp.float32)
    for at, factor in enumerate((current, scaled)):
        left = jnp.sum(factor * current, axis=1, keepdims=True)
        for term in range(3):
            head = left.astype(jnp.bfloat16).astype(jnp.float32)
            table = jnp.where(lane == 3 * at + term, head, table)
            left = left - head
    table = jnp.concatenate([table, jnp.zeros((128 - rows, 128), jnp.float32)], axis=0)
    sums = jnp.broadcast_to(table.T[None, :8], (rows // 8, 8, 128))

    low, high = regroup(*tiles[:2]), regroup(*tiles[2:])
    for parity in range(2):
        sides = [
            part[parity][:, :, at : at + 128] for at in range(0, width, 128) for part in (low, high)
        ]
        out_ref[:, parity] = jnp.concatenate(sides + [sums], axis=1).astype(out_ref.dtype)


def cascade(parts, start):
    _, rows, width = parts.shape
    half = jax.ShapeDtypeStruct((rows, width), jnp.float32)
    out, final, scaled = call(
        cascade_kernel,
        "cascade",
        parts.size,
        2 * parts.size,
        out_shape=(jax.ShapeDtypeStruct((rows // 8, 2, 40, 128), jnp.bfloat16), half, half),
    )(parts, start)
    return out.reshape(rows // 4, 40, 128), final, scaled


def norm_kernel(core_ref, got_ref, final_ref, scaled_ref, out_ref):
    planes = got_ref.shape[0]
    rows, width = final_ref.shape
    sums = got_ref[0, 32:40].astype(jnp.float32)
    for plane in range(1, planes):
        sums += got_ref[plane, 32:40].astype(jnp.float32)
    table = jnp.concatenate([sums, jnp.zeros((120, 128), jnp.float32)], axis=0).T[:rows]
    lane = lax.broadcasted_iota(jnp.int32, table.shape, 1)
    square = jnp.sum(jnp.where(lane < 3, table, 0.0), axis=1, keepdims=True) / D
    mixed = jnp.sum(jnp.where(lane < 3, 0.0, table), axis=1, keepdims=True) / D
    inverse = lax.rsqrt(square + 1e-05)
    grad = inverse * (scaled_ref[...] - final_ref[...] * (inverse * inverse * mixed))

    shards = planes // 2
    first = core_ref[0] == 0
    spread = jnp.broadcast_to(grad[None], (shards // 2, rows, width))
    pairs = got_ref[...].astype(jnp.float32).reshape(shards, 2, 40, 128)
    for at in range(2):
        even, odd = (
            jnp.concatenate([pairs[:, q, row : row + 8] for row in (8 * at, 8 * at + 16)], axis=2)
            for q in range(2)
        )
        for parity, tile in enumerate(regroup(even, odd)):
            tile = tile.reshape(shards // 2, 2, 8, width)
            same = jnp.where(first, tile[:, 0], tile[:, 1])
            other = jnp.where(first, tile[:, 1], tile[:, 0])
            joined = jnp.concatenate([spread, same, other], axis=1)
            out_ref[2 * at + parity] = joined.astype(out_ref.dtype)


def norm(core, got, final, scaled):
    rows, width = final.shape
    chips = got.shape[0] // 4
    whole = pl.BlockSpec(memory_space=pltpu.VMEM)
    out = call(
        norm_kernel,
        "norm_gradient",
        got.size,
        4 * got.size,
        in_specs=[pl.BlockSpec(memory_space=pltpu.SMEM), whole, whole, whole],
        out_specs=whole,
        out_shape=jax.ShapeDtypeStruct((4, chips, rows + 16, width), jnp.bfloat16),
    )(core, got, final, scaled)
    return out.reshape(4 * chips, rows + 16, width)


def products(core, full_ref, acts_ref, turned_ref, section_at):
    groups, _, rows, units = acts_ref.shape
    _, tiles, _, width = full_ref.shape

    def regrouped(at):
        even = full_ref[0, :, at : at + 8].astype(jnp.float32)
        odd = full_ref[1, :, at : at + 8].astype(jnp.float32)
        return [t.reshape(8 * tiles, width) for t in regroup(even, odd)]

    for two in range(groups // 2):
        pair = jnp.concatenate(regrouped(8 * two), axis=0)
        at = 2 * two * rows
        turned_ref[:, at : at + 2 * rows] = pair.T.astype(turned_ref.dtype)
    found = None
    for step in range(2):
        part = groups // 2
        acts = acts_ref[step * part : (step + 1) * part, core].reshape(part * rows, units)
        term = jnp.dot(
            turned_ref[:, step * part * rows : (step + 1) * part * rows],
            acts,
            preferred_element_type=jnp.float32,
        )
        found = term if found is None else found + term
    return found, jnp.concatenate(regrouped(section_at), axis=1)


def near_kernel(core_ref, full_ref, acts_ref, found_ref, section_ref, turned_ref):
    rows = full_ref.shape[2]
    found, section = products(core_ref[0], full_ref, acts_ref, turned_ref, rows - 16)
    found_ref[...] = found
    section_ref[...] = section.astype(section_ref.dtype)


def far_kernel(
    core_ref,
    kept_ref,
    full_ref,
    acts_ref,
    near_ref,
    near_section_ref,
    out_ref,
    section_ref,
    turned_ref,
    found_ref,
):
    cols, keep, blk, _ = out_ref.shape
    core, rows = core_ref[0], full_ref.shape[2]
    found, section = products(1 - core, full_ref, acts_ref, turned_ref, rows - 8)
    half = section_ref.shape[0] // 2
    section_ref[pl.ds(pl.multiple_of(core * half, half), half)] = near_section_ref[...]
    section_ref[pl.ds(pl.multiple_of((1 - core) * half, half), half)] = section.astype(
        section_ref.dtype
    )
    found_ref[...] = (near_ref[...] + found).astype(found_ref.dtype)
    for c in range(cols):
        for slot in range(keep):
            start = pl.multiple_of(kept_ref[c, slot] * blk, blk)
            out_ref[c, slot] = found_ref[c * blk : (c + 1) * blk, pl.ds(start, blk)].T


def gradient(core, own_kept, full, held, blk):
    groups, _, rows, units = held.shape
    chips, _, width = full.shape
    cols, keep = own_kept.shape
    full = full.reshape(2, chips // 2, *full.shape[1:])
    whole = pl.BlockSpec(memory_space=pltpu.VMEM)
    scalar = pl.BlockSpec(memory_space=pltpu.SMEM)
    turned = pltpu.VMEM((width, groups * rows), jnp.bfloat16)
    flops = 2 * groups * rows * units * width
    other = lax.ppermute(full, "core", [(0, 1), (1, 0)])
    found, section = call(
        near_kernel,
        "own_core_gradient",
        flops,
        held.size,
        in_specs=[scalar, whole, whole],
        out_specs=[whole, whole],
        scratch_shapes=[turned],
        out_shape=(
            jax.ShapeDtypeStruct((width, units), jnp.float32),
            jax.ShapeDtypeStruct((rows, 2 * width), jnp.bfloat16),
        ),
    )(core, full, held)
    return call(
        far_kernel,
        "other_core_gradient",
        flops,
        held.size,
        in_specs=[scalar, scalar] + [whole] * 4,
        out_specs=[whole, whole],
        scratch_shapes=[turned, pltpu.VMEM((width, units), jnp.bfloat16)],
        out_shape=(
            jax.ShapeDtypeStruct((cols, keep, blk, blk), jnp.bfloat16),
            jax.ShapeDtypeStruct((2 * rows, 2 * width), jnp.bfloat16),
        ),
    )(core, own_kept, other, held, found, section)


def exchange(value, axes):
    return lax.all_to_all(value, axes, split_axis=0, concat_axis=0, tiled=True)


def body(hidden, residual_in, weights, kept, cotangent, norm_gain):
    nz = lax.axis_size("dp")
    core = lax.axis_index("core").astype(jnp.int32).reshape(1)
    section, plane = lax.axis_index("section"), lax.axis_index("dp")
    acts = hidden[0]
    rows = acts.shape[0]
    blocks = weights[0, 0]
    cols, _, blk, _ = blocks.shape
    width = cols * blk
    hidden_blocks = acts.shape[1] // blk
    every = lax.all_gather(acts, "dp", axis=0, tiled=True)
    own_kept = lax.dynamic_slice_in_dim(kept[0, 0], plane * cols, cols, axis=0)
    hit = own_kept[None] == jnp.arange(hidden_blocks, dtype=own_kept.dtype)[:, None, None]
    dense = jnp.sum(
        jnp.where(hit[..., None, None], blocks[None].astype(jnp.float32), 0.0), axis=2
    ).astype(jnp.bfloat16)
    dense = dense.transpose(0, 2, 1, 3).reshape(hidden_blocks * blk, width)

    pairs = to_columns(lax.axis_size("section"), nz, lax.axis_size("x"))
    start = split(section, residual_in, cotangent, norm_gain)
    start = lax.ppermute(start, ("section", "dp") + TENSOR, pairs)
    start = exchange(start, CHIPS)
    partial_out, held = forward(core, every, dense, rows, start)
    sent, final, scaled = cascade(exchange(partial_out, CHIPS), start)
    spread = norm(core, exchange(sent, "dp"), final, scaled)
    grads, section_out = gradient(core, own_kept, exchange(spread, CHIPS), held, blk)
    return (section_out[None], grads[None, None])


def solution(mesh):
    sizes = mesh.shape
    shape = (sizes["section"], sizes["dp"], sizes["tensor"] // 2, 2)
    chips = Mesh(mesh.devices.reshape(shape), ("section", "dp") + TENSOR)
    in_specs = (
        P("section", "dp", TENSOR),
        P("dp", TENSOR),
        P("section", TENSOR, "dp", None, None, None),
        P("section", TENSOR, None, None),
        P("dp", TENSOR),
        P(TENSOR),
    )
    out_specs = (P("section", "dp", TENSOR), P("section", TENSOR, "dp", None, None, None))
    return jax.shard_map(body, mesh=chips, in_specs=in_specs, out_specs=out_specs, check_vma=False)
```

```python
import jax
import jax.numpy as jnp
from jax import lax
from jax.experimental import pallas as pl
from jax.experimental.pallas import tpu as pltpu
from jax.sharding import Mesh
from jax.sharding import PartitionSpec as P

D = 4096
TENSOR = ("x", "core")
CHIPS = ("section", "x")
HALF = 4


def regroup(even, odd):
    upper = lax.broadcasted_iota(jnp.int32, even.shape, even.ndim - 2) < HALF
    axis = even.ndim - 2
    first = jnp.where(upper, even, pltpu.roll(odd, HALF, axis))
    second = jnp.where(upper, pltpu.roll(even, HALF, axis), odd)
    return first, second


def call(kernel, name, flops, moved, vmem=16 << 20, **kwargs):
    return pl.pallas_call(
        kernel,
        compiler_params=pltpu.CompilerParams(vmem_limit_bytes=vmem),
        cost_estimate=pl.CostEstimate(flops=flops, bytes_accessed=moved, transcendentals=0),
        name=name,
        **kwargs,
    )


def split_kernel(section_ref, residual_ref, cot_ref, gain_ref, out_ref):
    rows, width = residual_ref.shape
    shape = (rows // 8, 8, width)
    scaled = cot_ref[...].astype(jnp.float32) * gain_ref[...]
    tiles = regroup(residual_ref[...].astype(jnp.float32).reshape(shape), scaled.reshape(shape))
    for half in range(2):
        out_ref[half] = tiles[half].astype(out_ref.dtype)


def split(section, residual, cotangent, gain):
    rows, width = residual.shape
    shape = (rows // 2, width // 2)
    block = pl.BlockSpec(shape, lambda i, s: (s[0] // 2, lax.rem(s[0], 2)))
    out = call(
        split_kernel,
        "split_rows",
        rows * width,
        2 * rows * width,
        grid_spec=pltpu.PrefetchScalarGridSpec(
            num_scalar_prefetch=1,
            grid=(1,),
            in_specs=[
                block,
                block,
                pl.BlockSpec((1, shape[1]), lambda i, s: (0, lax.rem(s[0], 2))),
            ],
            out_specs=pl.BlockSpec((2, rows // 16, 8, shape[1]), lambda i, s: (0,) * 4),
        ),
        out_shape=jax.ShapeDtypeStruct((2, rows // 16, 8, shape[1]), jnp.bfloat16),
    )(section.astype(jnp.int32).reshape(1), residual, cotangent, gain.reshape(1, width))
    return out.reshape(rows // 8, 8, shape[1])


def to_columns(ns, nz, nx):
    pairs = []
    for s in range(ns):
        for z in range(nz):
            for t in range(2 * nx):
                source = (s * nz + z) * 2 * nx + t
                plane = 2 * t + s % 2
                pairs.append((source, ((z // nx * nz + plane) * nx + z % nx) * 2 + s // 2))
    return pairs


def partial_sums(core, acts_ref, dense_ref, out_ref, held_ref):
    groups, _, rows, units = acts_ref.shape
    width = dense_ref.shape[1]
    for step in range(groups // 8):
        acts = acts_ref[8 * step : 8 * step + 8, core]
        held_ref[8 * step : 8 * step + 8] = acts
        found = jnp.dot(
            acts.reshape(8 * rows, units), dense_ref[...], preferred_element_type=jnp.float32
        )
        found = found.reshape(8, rows // 8, 8, width)
        pairs = [regroup(found[2 * q], found[2 * q + 1]) for q in range(4)]
        at = slice(32 * step, 32 * step + 32)
        for half in range(2):
            joined = jnp.concatenate([pair[half] for pair in pairs], axis=1)
            out_ref[half, :, at] = joined.astype(out_ref.dtype)


def other_kernel(core_ref, acts_ref, dense_ref, after_ref, out_ref, held_ref):
    partial_sums(1 - core_ref[0], acts_ref, dense_ref, out_ref, held_ref)


def own_kernel(core_ref, acts_ref, dense_ref, out_ref, held_ref):
    partial_sums(core_ref[0], acts_ref, dense_ref, out_ref, held_ref)


def add_kernel(own_ref, got_ref, out_ref):
    out_ref[...] = (own_ref[...] + got_ref[...].astype(jnp.float32)).astype(out_ref.dtype)


def forward(core, every, dense, rows, after):
    tokens, units = every.shape
    width = dense.shape[1]
    groups = tokens // rows
    every = every.reshape(groups, 2, rows // 2, units)
    held = pltpu.VMEM((groups, rows // 2, units), every.dtype)
    out = jax.ShapeDtypeStruct((2, rows // 16, HALF * groups, width), jnp.bfloat16)
    whole = pl.BlockSpec(memory_space=pltpu.VMEM)
    scalar = pl.BlockSpec(memory_space=pltpu.SMEM)
    sent, others = call(
        other_kernel,
        "other_core_matmul",
        tokens * units * width,
        2 * tokens * units,
        in_specs=[scalar, whole, whole, pl.BlockSpec(memory_space=pl.ANY)],
        out_specs=[whole, whole],
        out_shape=(out, held),
    )(core, every, dense, after)
    got = lax.ppermute(sent, "core", [(0, 1), (1, 0)])
    own, mine = call(
        own_kernel,
        "own_core_matmul",
        tokens * units * width,
        tokens * units,
        in_specs=[scalar, whole, whole],
        out_specs=[whole, whole],
        out_shape=(jax.ShapeDtypeStruct(out.shape, jnp.float32), held),
    )(core, every, dense)
    both = call(
        add_kernel,
        "add_cores",
        out.size,
        8 * out.size,
        in_specs=[whole] * 2,
        out_specs=whole,
        out_shape=out,
    )(own, got)
    return both.reshape(rows // 8, HALF * groups, width), mine, others


def cascade_kernel(parts_ref, start_ref, out_ref, final_ref, scaled_ref):
    rows, width = final_ref.shape
    shards = parts_ref.shape[0] // 4
    start = start_ref[...].astype(jnp.float32).reshape(rows // 8, 2, 8, width)
    current, scaled = (t.reshape(rows, width) for t in regroup(start[:, 0], start[:, 1]))
    tiles = []
    for section in range(4):
        contrib = parts_ref[section * shards].astype(jnp.float32)
        for shard in range(1, shards):
            contrib += parts_ref[section * shards + shard].astype(jnp.float32)
        current = (current + contrib).astype(jnp.bfloat16).astype(jnp.float32)
        tiles.append(current.reshape(rows // 8, 8, width))
    final_ref[...] = current
    scaled_ref[...] = scaled

    lane = lax.broadcasted_iota(jnp.int32, (rows, 128), 1)
    table = jnp.zeros((rows, 128), jnp.float32)
    for at, factor in enumerate((current, scaled)):
        left = jnp.sum(factor * current, axis=1, keepdims=True)
        for term in range(3):
            head = left.astype(jnp.bfloat16).astype(jnp.float32)
            table = jnp.where(lane == 3 * at + term, head, table)
            left = left - head
    table = jnp.concatenate([table, jnp.zeros((128 - rows, 128), jnp.float32)], axis=0)
    sums = jnp.broadcast_to(table.T[None, :8], (rows // 8, 8, 128))

    low, high = regroup(*tiles[:2]), regroup(*tiles[2:])
    for parity in range(2):
        sides = [
            part[parity][:, :, at : at + 128] for at in range(0, width, 128) for part in (low, high)
        ]
        out_ref[:, parity] = jnp.concatenate(sides + [sums], axis=1).astype(out_ref.dtype)


def cascade(parts, start):
    _, rows, width = parts.shape
    half = jax.ShapeDtypeStruct((rows, width), jnp.float32)
    out, final, scaled = call(
        cascade_kernel,
        "cascade",
        parts.size,
        2 * parts.size,
        out_shape=(jax.ShapeDtypeStruct((rows // 8, 2, 40, 128), jnp.bfloat16), half, half),
    )(parts, start)
    return out.reshape(rows // 4, 40, 128), final, scaled


def norm_kernel(core_ref, got_ref, final_ref, scaled_ref, out_ref):
    planes = got_ref.shape[0]
    rows, width = final_ref.shape
    sums = got_ref[0, 32:40].astype(jnp.float32)
    for plane in range(1, planes):
        sums += got_ref[plane, 32:40].astype(jnp.float32)
    table = jnp.concatenate([sums, jnp.zeros((120, 128), jnp.float32)], axis=0).T[:rows]
    lane = lax.broadcasted_iota(jnp.int32, table.shape, 1)
    square = jnp.sum(jnp.where(lane < 3, table, 0.0), axis=1, keepdims=True) / D
    mixed = jnp.sum(jnp.where(lane < 3, 0.0, table), axis=1, keepdims=True) / D
    inverse = lax.rsqrt(square + 1e-05)
    grad = inverse * (scaled_ref[...] - final_ref[...] * (inverse * inverse * mixed))

    shards = planes // 2
    first = core_ref[0] == 0
    spread = jnp.broadcast_to(grad[None], (shards // 2, rows, width))
    pairs = got_ref[...].astype(jnp.float32).reshape(shards, 2, 40, 128)
    for at in range(2):
        even, odd = (
            jnp.concatenate([pairs[:, q, row : row + 8] for row in (8 * at, 8 * at + 16)], axis=2)
            for q in range(2)
        )
        for parity, tile in enumerate(regroup(even, odd)):
            tile = tile.reshape(shards // 2, 2, 8, width)
            same = jnp.where(first, tile[:, 0], tile[:, 1])
            other = jnp.where(first, tile[:, 1], tile[:, 0])
            joined = jnp.concatenate([spread, same, other], axis=1)
            out_ref[2 * at + parity] = joined.astype(out_ref.dtype)


def norm(core, got, final, scaled):
    rows, width = final.shape
    chips = got.shape[0] // 4
    whole = pl.BlockSpec(memory_space=pltpu.VMEM)
    out = call(
        norm_kernel,
        "norm_gradient",
        got.size,
        4 * got.size,
        in_specs=[pl.BlockSpec(memory_space=pltpu.SMEM), whole, whole, whole],
        out_specs=whole,
        out_shape=jax.ShapeDtypeStruct((4, chips, rows + 16, width), jnp.bfloat16),
    )(core, got, final, scaled)
    return out.reshape(4 * chips, rows + 16, width)


def products(full_ref, acts_ref, turned_ref, section_at):
    groups, rows, units = acts_ref.shape
    _, tiles, _, width = full_ref.shape

    def regrouped(at):
        even = full_ref[0, :, at : at + 8].astype(jnp.float32)
        odd = full_ref[1, :, at : at + 8].astype(jnp.float32)
        return [t.reshape(8 * tiles, width) for t in regroup(even, odd)]

    for two in range(groups // 2):
        pair = jnp.concatenate(regrouped(8 * two), axis=0)
        at = 2 * two * rows
        turned_ref[:, at : at + 2 * rows] = pair.T.astype(turned_ref.dtype)
    found = None
    for step in range(2):
        part = groups // 2
        acts = acts_ref[step * part : (step + 1) * part].reshape(part * rows, units)
        term = jnp.dot(
            turned_ref[:, step * part * rows : (step + 1) * part * rows],
            acts,
            preferred_element_type=jnp.float32,
        )
        found = term if found is None else found + term
    return found, jnp.concatenate(regrouped(section_at), axis=1)


def near_kernel(full_ref, acts_ref, found_ref, section_ref, turned_ref):
    rows = full_ref.shape[2]
    found, section = products(full_ref, acts_ref, turned_ref, rows - 16)
    found_ref[...] = found
    section_ref[...] = section.astype(section_ref.dtype)


def far_kernel(
    core_ref,
    kept_ref,
    full_ref,
    acts_ref,
    near_ref,
    near_section_ref,
    out_ref,
    section_out_ref,
    turned_ref,
    found_ref,
    blocks_ref,
    section_ref,
    sems,
):
    cols, keep, blk, _ = out_ref.shape
    copies = [pltpu.make_async_copy(section_ref, section_out_ref, sems.at[cols])]
    for c in range(cols):
        copies.append(pltpu.make_async_copy(blocks_ref.at[c], out_ref.at[c], sems.at[c]))
    core, rows = core_ref[0], full_ref.shape[2]
    found, section = products(full_ref, acts_ref, turned_ref, rows - 8)
    half = section_ref.shape[0] // 2
    section_ref[pl.ds(pl.multiple_of(core * half, half), half)] = near_section_ref[...]
    section_ref[pl.ds(pl.multiple_of((1 - core) * half, half), half)] = section.astype(
        section_ref.dtype
    )
    copies[0].start()
    found_ref[...] = (near_ref[...] + found).astype(found_ref.dtype)
    for c in range(cols):
        for slot in range(keep):
            start = pl.multiple_of(kept_ref[c, slot] * blk, blk)
            blocks_ref[c, slot] = found_ref[c * blk : (c + 1) * blk, pl.ds(start, blk)].T
        copies[1 + c].start()
    for copy in copies:
        copy.wait()


def gradient(core, own_kept, full, mine, others, blk):
    groups, rows, units = mine.shape
    chips, _, width = full.shape
    cols, keep = own_kept.shape
    full = full.reshape(2, chips // 2, *full.shape[1:])
    whole = pl.BlockSpec(memory_space=pltpu.VMEM)
    scalar = pl.BlockSpec(memory_space=pltpu.SMEM)
    turned = pltpu.VMEM((width, groups * rows), jnp.bfloat16)
    flops = 2 * groups * rows * units * width
    other = lax.ppermute(full, "core", [(0, 1), (1, 0)])
    found, section = call(
        near_kernel,
        "own_core_gradient",
        flops,
        2 * mine.size,
        in_specs=[whole, whole],
        out_specs=[whole, whole],
        scratch_shapes=[turned],
        out_shape=(
            jax.ShapeDtypeStruct((width, units), jnp.float32),
            jax.ShapeDtypeStruct((rows, 2 * width), jnp.bfloat16),
        ),
    )(full, mine)
    return call(
        far_kernel,
        "other_core_gradient",
        flops,
        2 * mine.size,
        in_specs=[scalar, scalar] + [whole] * 4,
        out_specs=[pl.BlockSpec(memory_space=pl.ANY)] * 2,
        scratch_shapes=[
            turned,
            pltpu.VMEM((width, units), jnp.bfloat16),
            pltpu.VMEM((cols, keep, blk, blk), jnp.bfloat16),
            pltpu.VMEM((2 * rows, 2 * width), jnp.bfloat16),
            pltpu.SemaphoreType.DMA((cols + 1,)),
        ],
        out_shape=(
            jax.ShapeDtypeStruct((cols, keep, blk, blk), jnp.bfloat16),
            jax.ShapeDtypeStruct((2 * rows, 2 * width), jnp.bfloat16),
        ),
    )(core, own_kept, other, others, found, section)


def exchange(value, axes):
    return lax.all_to_all(value, axes, split_axis=0, concat_axis=0, tiled=True)


def body(hidden, residual_in, weights, kept, cotangent, norm_gain):
    nz = lax.axis_size("dp")
    core = lax.axis_index("core").astype(jnp.int32).reshape(1)
    section, plane = lax.axis_index("section"), lax.axis_index("dp")
    acts = hidden[0]
    rows = acts.shape[0]
    blocks = weights[0, 0]
    cols, _, blk, _ = blocks.shape
    width = cols * blk
    hidden_blocks = acts.shape[1] // blk
    every = lax.all_gather(acts, "dp", axis=0, tiled=True)
    own_kept = lax.dynamic_slice_in_dim(kept[0, 0], plane * cols, cols, axis=0)
    hit = own_kept[None] == jnp.arange(hidden_blocks, dtype=own_kept.dtype)[:, None, None]
    dense = jnp.sum(
        jnp.where(hit[..., None, None], blocks[None].astype(jnp.float32), 0.0), axis=2
    ).astype(jnp.bfloat16)
    dense = dense.transpose(0, 2, 1, 3).reshape(hidden_blocks * blk, width)

    pairs = to_columns(lax.axis_size("section"), nz, lax.axis_size("x"))
    start = split(section, residual_in, cotangent, norm_gain)
    start = lax.ppermute(start, ("section", "dp") + TENSOR, pairs)
    start = exchange(start, CHIPS)
    partial_out, mine, others = forward(core, every, dense, rows, start)
    sent, final, scaled = cascade(exchange(partial_out, CHIPS), start)
    spread = norm(core, exchange(sent, "dp"), final, scaled)
    grads, section_out = gradient(core, own_kept, exchange(spread, CHIPS), mine, others, blk)
    return (section_out[None], grads[None, None])


def solution(mesh):
    sizes = mesh.shape
    shape = (sizes["section"], sizes["dp"], sizes["tensor"] // 2, 2)
    chips = Mesh(mesh.devices.reshape(shape), ("section", "dp") + TENSOR)
    in_specs = (
        P("section", "dp", TENSOR),
        P("dp", TENSOR),
        P("section", TENSOR, "dp", None, None, None),
        P("section", TENSOR, None, None),
        P("dp", TENSOR),
        P(TENSOR),
    )
    out_specs = (P("section", "dp", TENSOR), P("section", TENSOR, "dp", None, None, None))
    return jax.shard_map(body, mesh=chips, in_specs=in_specs, out_specs=out_specs, check_vma=False)
```

```python
import jax
import jax.numpy as jnp
from jax import lax
from jax.experimental import pallas as pl
from jax.experimental.pallas import tpu as pltpu
from jax.sharding import Mesh
from jax.sharding import PartitionSpec as P

D = 4096
TENSOR = ("x", "core")
CHIPS = ("section", "x")
TURNED = ("x", "section")
HALF = 4


def regroup(even, odd):
    upper = lax.broadcasted_iota(jnp.int32, even.shape, even.ndim - 2) < HALF
    axis = even.ndim - 2
    first = jnp.where(upper, even, pltpu.roll(odd, HALF, axis))
    second = jnp.where(upper, pltpu.roll(even, HALF, axis), odd)
    return first, second


def call(kernel, name, flops, moved, vmem=16 << 20, **kwargs):
    return pl.pallas_call(
        kernel,
        compiler_params=pltpu.CompilerParams(vmem_limit_bytes=vmem),
        cost_estimate=pl.CostEstimate(flops=flops, bytes_accessed=moved, transcendentals=0),
        name=name,
        **kwargs,
    )


def split_kernel(section_ref, residual_ref, cot_ref, gain_ref, out_ref):
    rows, width = residual_ref.shape
    shape = (rows // 8, 8, width)
    scaled = cot_ref[...].astype(jnp.float32) * gain_ref[...]
    tiles = regroup(residual_ref[...].astype(jnp.float32).reshape(shape), scaled.reshape(shape))
    for half in range(2):
        out_ref[half] = tiles[half].astype(out_ref.dtype)


def split(section, residual, cotangent, gain):
    rows, width = residual.shape
    shape = (rows // 2, width // 2)
    block = pl.BlockSpec(shape, lambda i, s: (s[0] // 2, lax.rem(s[0], 2)))
    out = call(
        split_kernel,
        "split_rows",
        rows * width,
        2 * rows * width,
        grid_spec=pltpu.PrefetchScalarGridSpec(
            num_scalar_prefetch=1,
            grid=(1,),
            in_specs=[
                block,
                block,
                pl.BlockSpec((1, shape[1]), lambda i, s: (0, lax.rem(s[0], 2))),
            ],
            out_specs=pl.BlockSpec((2, rows // 16, 8, shape[1]), lambda i, s: (0,) * 4),
        ),
        out_shape=jax.ShapeDtypeStruct((2, rows // 16, 8, shape[1]), jnp.bfloat16),
    )(section.astype(jnp.int32).reshape(1), residual, cotangent, gain.reshape(1, width))
    return out.reshape(rows // 8, 8, shape[1])


def to_columns(ns, nz, nx):
    pairs = []
    for s in range(ns):
        for z in range(nz):
            for t in range(2 * nx):
                source = (s * nz + z) * 2 * nx + t
                plane = 2 * t + s % 2
                pairs.append((source, ((z // nx * nz + plane) * nx + z % nx) * 2 + s // 2))
    return pairs


def partial_sums(core, acts_ref, dense_ref, out_ref, held_ref):
    groups, _, rows, units = acts_ref.shape
    width = dense_ref.shape[1]
    for step in range(groups // 8):
        acts = acts_ref[8 * step : 8 * step + 8, core]
        held_ref[8 * step : 8 * step + 8] = acts
        found = jnp.dot(
            acts.reshape(8 * rows, units), dense_ref[...], preferred_element_type=jnp.float32
        )
        found = found.reshape(8, rows // 8, 8, width)
        pairs = [regroup(found[2 * q], found[2 * q + 1]) for q in range(4)]
        at = slice(32 * step, 32 * step + 32)
        for half in range(2):
            joined = jnp.concatenate([pair[half] for pair in pairs], axis=1)
            out_ref[half, :, at] = joined.astype(out_ref.dtype)


def other_kernel(core_ref, acts_ref, dense_ref, after_ref, out_ref, held_ref):
    partial_sums(1 - core_ref[0], acts_ref, dense_ref, out_ref, held_ref)


def own_kernel(core_ref, acts_ref, dense_ref, out_ref, held_ref):
    partial_sums(core_ref[0], acts_ref, dense_ref, out_ref, held_ref)


def add_kernel(own_ref, got_ref, out_ref):
    both = (own_ref[...] + got_ref[...].astype(jnp.float32)).astype(out_ref.dtype)
    chips = out_ref.shape[0]
    for half in range(2):
        for part in range(2):
            out_ref[:, half, part] = both[half, part * chips : (part + 1) * chips]


def forward(core, every, dense, rows, after):
    tokens, units = every.shape
    width = dense.shape[1]
    groups = tokens // rows
    every = every.reshape(groups, 2, rows // 2, units)
    held = pltpu.VMEM((groups, rows // 2, units), every.dtype)
    out = jax.ShapeDtypeStruct((2, rows // 16, HALF * groups, width), jnp.bfloat16)
    whole = pl.BlockSpec(memory_space=pltpu.VMEM)
    scalar = pl.BlockSpec(memory_space=pltpu.SMEM)
    sent, others = call(
        other_kernel,
        "other_core_matmul",
        tokens * units * width,
        2 * tokens * units,
        in_specs=[scalar, whole, whole, pl.BlockSpec(memory_space=pl.ANY)],
        out_specs=[whole, whole],
        out_shape=(out, held),
    )(core, every, dense, after)
    got = lax.ppermute(sent, "core", [(0, 1), (1, 0)])
    own, mine = call(
        own_kernel,
        "own_core_matmul",
        tokens * units * width,
        tokens * units,
        in_specs=[scalar, whole, whole],
        out_specs=[whole, whole],
        out_shape=(jax.ShapeDtypeStruct(out.shape, jnp.float32), held),
    )(core, every, dense)
    both = call(
        add_kernel,
        "add_cores",
        out.size,
        8 * out.size,
        in_specs=[whole] * 2,
        out_specs=whole,
        out_shape=jax.ShapeDtypeStruct((out.shape[1] // 2, 2, 2, *out.shape[2:]), out.dtype),
    )(own, got)
    return both.reshape(rows // 8, HALF * groups, width), mine, others


def cascade_kernel(parts_ref, start_ref, out_ref, final_ref, scaled_ref):
    rows, width = final_ref.shape
    shards = parts_ref.shape[0] // 4
    start = start_ref[...].astype(jnp.float32).reshape(rows // 8, 2, 8, width)
    current, scaled = (t.reshape(rows, width) for t in regroup(start[:, 0], start[:, 1]))
    tiles = []
    for section in range(4):
        contrib = parts_ref[section].astype(jnp.float32)
        for shard in range(1, shards):
            contrib += parts_ref[4 * shard + section].astype(jnp.float32)
        current = (current + contrib).astype(jnp.bfloat16).astype(jnp.float32)
        tiles.append(current.reshape(rows // 8, 8, width))
    final_ref[...] = current
    scaled_ref[...] = scaled

    lane = lax.broadcasted_iota(jnp.int32, (rows, 128), 1)
    table = jnp.zeros((rows, 128), jnp.float32)
    for at, factor in enumerate((current, scaled)):
        left = jnp.sum(factor * current, axis=1, keepdims=True)
        for term in range(3):
            head = left.astype(jnp.bfloat16).astype(jnp.float32)
            table = jnp.where(lane == 3 * at + term, head, table)
            left = left - head
    table = jnp.concatenate([table, jnp.zeros((128 - rows, 128), jnp.float32)], axis=0)
    sums = jnp.broadcast_to(table.T[None, :8], (rows // 8, 8, 128))

    low, high = regroup(*tiles[:2]), regroup(*tiles[2:])
    for parity in range(2):
        sides = [
            part[parity][:, :, at : at + 128] for at in range(0, width, 128) for part in (low, high)
        ]
        out_ref[:, parity] = jnp.concatenate(sides + [sums], axis=1).astype(out_ref.dtype)


def cascade(parts, start):
    _, rows, width = parts.shape
    half = jax.ShapeDtypeStruct((rows, width), jnp.float32)
    out, final, scaled = call(
        cascade_kernel,
        "cascade",
        parts.size,
        2 * parts.size,
        out_shape=(jax.ShapeDtypeStruct((rows // 8, 2, 40, 128), jnp.bfloat16), half, half),
    )(parts, start)
    return out.reshape(rows // 4, 40, 128), final, scaled


def norm_kernel(core_ref, got_ref, final_ref, scaled_ref, out_ref):
    planes = got_ref.shape[0]
    rows, width = final_ref.shape
    sums = got_ref[0, 32:40].astype(jnp.float32)
    for plane in range(1, planes):
        sums += got_ref[plane, 32:40].astype(jnp.float32)
    table = jnp.concatenate([sums, jnp.zeros((120, 128), jnp.float32)], axis=0).T[:rows]
    lane = lax.broadcasted_iota(jnp.int32, table.shape, 1)
    square = jnp.sum(jnp.where(lane < 3, table, 0.0), axis=1, keepdims=True) / D
    mixed = jnp.sum(jnp.where(lane < 3, 0.0, table), axis=1, keepdims=True) / D
    inverse = lax.rsqrt(square + 1e-05)
    grad = inverse * (scaled_ref[...] - final_ref[...] * (inverse * inverse * mixed))

    shards = planes // 2
    first = core_ref[0] == 0
    spread = jnp.broadcast_to(grad[None], (shards // 2, rows, width))
    pairs = got_ref[...].astype(jnp.float32).reshape(shards, 2, 40, 128)
    for at in range(2):
        even, odd = (
            jnp.concatenate([pairs[:, q, row : row + 8] for row in (8 * at, 8 * at + 16)], axis=2)
            for q in range(2)
        )
        for parity, tile in enumerate(regroup(even, odd)):
            tile = tile.reshape(shards // 2, 2, 8, width)
            same = jnp.where(first, tile[:, 0], tile[:, 1])
            other = jnp.where(first, tile[:, 1], tile[:, 0])
            joined = jnp.concatenate([spread, same, other], axis=1)
            out_ref[:, 2 * at + parity] = joined.astype(out_ref.dtype)


def norm(core, got, final, scaled):
    rows, width = final.shape
    chips = got.shape[0] // 4
    whole = pl.BlockSpec(memory_space=pltpu.VMEM)
    out = call(
        norm_kernel,
        "norm_gradient",
        got.size,
        4 * got.size,
        in_specs=[pl.BlockSpec(memory_space=pltpu.SMEM), whole, whole, whole],
        out_specs=whole,
        out_shape=jax.ShapeDtypeStruct((chips, 4, rows + 16, width), jnp.bfloat16),
    )(core, got, final, scaled)
    return out.reshape(4 * chips, rows + 16, width)


def products(full_ref, acts_ref, turned_ref, section_at):
    groups, rows, units = acts_ref.shape
    tiles, width = 2 * full_ref.shape[0], full_ref.shape[4]

    def regrouped(at):
        even, odd = (
            jnp.concatenate(
                [full_ref[:, half, part, at : at + 8] for part in range(2)], axis=0
            ).astype(jnp.float32)
            for half in range(2)
        )
        return [t.reshape(8 * tiles, width) for t in regroup(even, odd)]

    for two in range(groups // 2):
        pair = jnp.concatenate(regrouped(8 * two), axis=0)
        at = 2 * two * rows
        turned_ref[:, at : at + 2 * rows] = pair.T.astype(turned_ref.dtype)
    found = None
    for step in range(2):
        part = groups // 2
        acts = acts_ref[step * part : (step + 1) * part].reshape(part * rows, units)
        term = jnp.dot(
            turned_ref[:, step * part * rows : (step + 1) * part * rows],
            acts,
            preferred_element_type=jnp.float32,
        )
        found = term if found is None else found + term
    return found, jnp.concatenate(regrouped(section_at), axis=1)


def near_kernel(full_ref, acts_ref, found_ref, section_ref, turned_ref):
    rows = full_ref.shape[3]
    found, section = products(full_ref, acts_ref, turned_ref, rows - 16)
    found_ref[...] = found
    section_ref[...] = section.astype(section_ref.dtype)


def far_kernel(
    core_ref,
    kept_ref,
    full_ref,
    acts_ref,
    near_ref,
    near_section_ref,
    out_ref,
    section_out_ref,
    turned_ref,
    found_ref,
    blocks_ref,
    section_ref,
    sems,
):
    cols, keep, blk, _ = out_ref.shape
    copies = [pltpu.make_async_copy(section_ref, section_out_ref, sems.at[cols])]
    for c in range(cols):
        copies.append(pltpu.make_async_copy(blocks_ref.at[c], out_ref.at[c], sems.at[c]))
    core, rows = core_ref[0], full_ref.shape[3]
    found, section = products(full_ref, acts_ref, turned_ref, rows - 8)
    half = section_ref.shape[0] // 2
    section_ref[pl.ds(pl.multiple_of(core * half, half), half)] = near_section_ref[...]
    section_ref[pl.ds(pl.multiple_of((1 - core) * half, half), half)] = section.astype(
        section_ref.dtype
    )
    copies[0].start()
    found_ref[...] = (near_ref[...] + found).astype(found_ref.dtype)
    for c in range(cols):
        for slot in range(keep):
            start = pl.multiple_of(kept_ref[c, slot] * blk, blk)
            blocks_ref[c, slot] = found_ref[c * blk : (c + 1) * blk, pl.ds(start, blk)].T
        copies[1 + c].start()
    for copy in copies:
        copy.wait()


def gradient(core, own_kept, full, mine, others, blk):
    groups, rows, units = mine.shape
    chips, _, width = full.shape
    cols, keep = own_kept.shape
    full = full.reshape(chips // 4, 2, 2, *full.shape[1:])
    whole = pl.BlockSpec(memory_space=pltpu.VMEM)
    scalar = pl.BlockSpec(memory_space=pltpu.SMEM)
    turned = pltpu.VMEM((width, groups * rows), jnp.bfloat16)
    flops = 2 * groups * rows * units * width
    other = lax.ppermute(full, "core", [(0, 1), (1, 0)])
    found, section = call(
        near_kernel,
        "own_core_gradient",
        flops,
        2 * mine.size,
        in_specs=[whole, whole],
        out_specs=[whole, whole],
        scratch_shapes=[turned],
        out_shape=(
            jax.ShapeDtypeStruct((width, units), jnp.float32),
            jax.ShapeDtypeStruct((rows, 2 * width), jnp.bfloat16),
        ),
    )(full, mine)
    return call(
        far_kernel,
        "other_core_gradient",
        flops,
        2 * mine.size,
        in_specs=[scalar, scalar] + [whole] * 4,
        out_specs=[pl.BlockSpec(memory_space=pl.ANY)] * 2,
        scratch_shapes=[
            turned,
            pltpu.VMEM((width, units), jnp.bfloat16),
            pltpu.VMEM((cols, keep, blk, blk), jnp.bfloat16),
            pltpu.VMEM((2 * rows, 2 * width), jnp.bfloat16),
            pltpu.SemaphoreType.DMA((cols + 1,)),
        ],
        out_shape=(
            jax.ShapeDtypeStruct((cols, keep, blk, blk), jnp.bfloat16),
            jax.ShapeDtypeStruct((2 * rows, 2 * width), jnp.bfloat16),
        ),
    )(core, own_kept, other, others, found, section)


def exchange(value, axes):
    return lax.all_to_all(value, axes, split_axis=0, concat_axis=0, tiled=True)


def body(hidden, residual_in, weights, kept, cotangent, norm_gain):
    nz = lax.axis_size("dp")
    core = lax.axis_index("core").astype(jnp.int32).reshape(1)
    section, plane = lax.axis_index("section"), lax.axis_index("dp")
    acts = hidden[0]
    rows = acts.shape[0]
    blocks = weights[0, 0]
    cols, _, blk, _ = blocks.shape
    width = cols * blk
    hidden_blocks = acts.shape[1] // blk
    every = lax.all_gather(acts, "dp", axis=0, tiled=True)
    own_kept = lax.dynamic_slice_in_dim(kept[0, 0], plane * cols, cols, axis=0)
    hit = own_kept[None] == jnp.arange(hidden_blocks, dtype=own_kept.dtype)[:, None, None]
    dense = jnp.sum(
        jnp.where(hit[..., None, None], blocks[None].astype(jnp.float32), 0.0), axis=2
    ).astype(jnp.bfloat16)
    dense = dense.transpose(0, 2, 1, 3).reshape(hidden_blocks * blk, width)

    pairs = to_columns(lax.axis_size("section"), nz, lax.axis_size("x"))
    start = split(section, residual_in, cotangent, norm_gain)
    start = lax.ppermute(start, ("section", "dp") + TENSOR, pairs)
    start = exchange(start, CHIPS)
    partial_out, mine, others = forward(core, every, dense, rows, start)
    sent, final, scaled = cascade(exchange(partial_out, TURNED), start)
    spread = norm(core, exchange(sent, "dp"), final, scaled)
    grads, section_out = gradient(core, own_kept, exchange(spread, TURNED), mine, others, blk)
    return (section_out[None], grads[None, None])


def solution(mesh):
    sizes = mesh.shape
    shape = (sizes["section"], sizes["dp"], sizes["tensor"] // 2, 2)
    chips = Mesh(mesh.devices.reshape(shape), ("section", "dp") + TENSOR)
    in_specs = (
        P("section", "dp", TENSOR),
        P("dp", TENSOR),
        P("section", TENSOR, "dp", None, None, None),
        P("section", TENSOR, None, None),
        P("dp", TENSOR),
        P(TENSOR),
    )
    out_specs = (P("section", "dp", TENSOR), P("section", TENSOR, "dp", None, None, None))
    return jax.shard_map(body, mesh=chips, in_specs=in_specs, out_specs=out_specs, check_vma=False)
```
